512 devices in a mesh: gx: 4 (over x), gy: 4 (over y), gz: 32 (over z, core).
Axes of the slice: x: 4, y: 4, z: 16, core: 2. Of those that a mesh axis runs over, the one named last changes fastest.
Arguments:
- substrate: float32 [128, 128, 512], P('gz', 'gx', 'gy'), may hold values from 0 to 2
- oxygen: float32 [128, 128, 512], P('gz', 'gx', 'gy'), may hold values from 0 to 1
- velocity: float32 [3, 128, 128, 512], P(None, 'gz', 'gx', 'gy'), may hold values from -0.2 to 0.2
- cell_map: int32 [128, 128, 512], P('gz', 'gx', 'gy'), may hold values from 0 to 8191, as said below
- owner_slot: int32 [8192], replicated, may hold values from 0 to 15871, as said below
- flow_list: int32 [2, 8192], replicated, may hold values from 0 to 8191, as said below
- flow_rates: float32 [16], replicated, may hold values from 0.05 to 0.4
- population: float32 [15872, 64, 256], P(('gx', 'gy', 'gz')), may hold values from 0.05 to 1
- growth: bfloat16 [256, 256], replicated, may hold values from -1 to 1
- daughter_kernel: bfloat16 [256, 256], replicated, may hold values from -1 to 1
- division_rate: float32 [64, 256], replicated, may hold values from 0.02 to 0.6
- uptake_weight: float32 [2, 256], replicated, may hold values from 0.1 to 1
Outputs:
- substrate_out: float32 [128, 128, 512], P('gz', 'gx', 'gy')
- oxygen_out: float32 [128, 128, 512], P('gz', 'gx', 'gy')
- population_out: float32 [15872, 64, 256], P(('gx', 'gy', 'gz'))
The draws below stay inside these ranges and needn't reach their ends.
Inputs may be any that keep to these rules, and one draw needn't show every extreme that they name: `cell_map`: every compartment holds exactly 1024 cells. `owner_slot`: distinct slots. The device with index d along gx+gy+gz holds slots d * 31 to d * 31 + 30, and its compartments fill a leading run of them, one at least. Two devices whose gz indices differ only in the lowest bit hold 32 compartments together. Some device holds 31. `flow_list`: A flow's target is owned by a device with the same gz index as its source's owner. From one device at most 2 flows go to the compartments of any one device, and some device sends 2 to some device.
All inputs are finite; a program needn't handle non-finite values.
Results may differ from the reference program's by a relative error of at most 0.0015.
The reference program's roundings to bfloat16 on the way count: a program that leaves them out, or rounds other values in their place, can miss the bound.
Values sent between devices are 32-bit elements; how exact they have to be, the bound alone decides.
A program may use at most 64 MiB of HBM per device.

```python
import math
import jax
import jax.numpy as jnp
from jax import lax

CX = 32
CY = 128
CZ = 4
COMP_DEV = 16
AGES = 64
SIZES = 256
SUBSTEPS = 8
RATES = 16
NX = 128
NY = 512
NZ = 128
COMPS = 8192
SLOTS = 31
CELLS = 1024
N_GX = 4
N_GY = 4
N_GZ = 32
DEVICES = 512


def spread_regions(region):
    return jnp.repeat(jnp.repeat(jnp.repeat(region, 2, axis=0), 4, axis=1), 8, axis=2)


def cell_field(region, key_cell):
    cells = jnp.exp(jax.random.uniform(key_cell, (NZ, NX, NY), jnp.float32, math.log(0.3), 0.0))
    return spread_regions(region) * cells


def draw_substrate(key, part):
    key = jax.random.fold_in(key, 11)
    key_region, key_cell = jax.random.split(key)
    shape = (NZ // 2, NX // 4, NY // 8)
    region = jnp.exp(jax.random.uniform(key_region, shape, jnp.float32, math.log(0.15), math.log(2.0)))
    return cell_field(region, key_cell)


def draw_oxygen(key, part):
    key = jax.random.fold_in(key, 13)
    key_region, key_cell = jax.random.split(key)
    shape = (NZ // 2, NX // 4, NY // 8)
    region = jnp.exp(jax.random.uniform(key_region, shape, jnp.float32, math.log(0.06), 0.0))
    return cell_field(region, key_cell)


def draw_cell_map(key, part):
    key = jax.random.fold_in(key, 23)
    key_one, key_two, key_three, key_four = jax.random.split(key, 4)
    box_x = CX // 2
    box_y = 2 * CY // COMP_DEV
    piece_z = CZ // 2
    shift_z = jax.random.randint(key_one, (), 0, piece_z)
    shift_y = jax.random.randint(key_two, (NZ, 1, 1), 0, box_y)
    shift_x = jax.random.randint(key_three, (NZ, 1, NY), 0, box_x)
    depth_pos = jnp.arange(NZ, dtype=jnp.int32)[:, None, None]
    row_pos = jnp.arange(NX, dtype=jnp.int32)[None, :, None]
    col_pos = jnp.arange(NY, dtype=jnp.int32)[None, None, :]
    layer_index = (depth_pos + shift_z) % NZ // piece_z
    row_index = (row_pos + shift_x) % NX // box_x
    col_index = (col_pos + shift_y) % NY // box_y
    piece = (layer_index * (NX // box_x) + row_index) * (NY // box_y) + col_index
    pairing = jax.random.permutation(key_four, 2 * COMPS).astype(jnp.int32)
    return (pairing[piece.astype(jnp.int32)] // 2).astype(jnp.int32)


def placement(key):
    key = jax.random.fold_in(key, 5)
    keys = jax.random.split(key, 6)
    pair_total = DEVICES // 2
    swing = jax.random.randint(keys[0], (pair_total,), 1 - COMP_DEV, COMP_DEV)
    chosen = jax.random.randint(keys[1], (), 0, pair_total)
    swing = jnp.where(jnp.arange(pair_total) == chosen, COMP_DEV - 1, swing)
    held = jnp.stack([COMP_DEV + swing, COMP_DEV - swing], axis=1).reshape(DEVICES).astype(jnp.int32)
    used_table = jnp.arange(SLOTS, dtype=jnp.int32)[None, :] < held[:, None]
    order = jnp.argsort(1 - used_table.reshape(-1).astype(jnp.int32), stable=True)
    used_slots = order[:COMPS].astype(jnp.int32)
    shuffle = jax.random.permutation(keys[2], COMPS)
    owner = used_slots[shuffle]
    comp_of_slot = jnp.zeros((DEVICES * SLOTS,), jnp.int32).at[owner].set(jnp.arange(COMPS, dtype=jnp.int32))
    positions = 2 * N_GX * N_GY
    scores = jax.random.randint(keys[3], (DEVICES, positions), 0, 1 << 20) * positions + jnp.arange(positions, dtype=jnp.int32)[None, :]
    device_perm = jnp.argsort(scores, axis=1).astype(jnp.int32)
    owner_dev = owner // SLOTS
    owner_local = owner % SLOTS
    column = device_perm[owner_dev, owner_local] // 2
    target_dev = column * N_GZ + owner_dev % N_GZ
    picked = jax.random.randint(keys[4], (COMPS,), 0, 1 << 20) % held[target_dev]
    target = comp_of_slot[target_dev * SLOTS + picked]
    rate_index = jax.random.randint(keys[5], (COMPS,), 0, RATES)
    return (owner.astype(jnp.int32), jnp.stack([target, rate_index]).astype(jnp.int32))


def draw_owner_slot(key, part):
    owner, flows = placement(key)
    return owner


def draw_flow_list(key, part):
    owner, flows = placement(key)
    return flows


def dominant(unit, diagonal, reach):
    eye_mask = jnp.eye(SIZES, dtype=bool)
    return jnp.where(eye_mask, diagonal, unit * (reach / SIZES))


def draw_growth(key, part):
    key = jax.random.fold_in(key, 31)
    unit = jax.random.uniform(key, (SIZES, SIZES), jnp.float32, -1.0, 1.0)
    return dominant(unit, 0.85, 0.7).astype(jnp.bfloat16)


def draw_daughter_kernel(key, part):
    key = jax.random.fold_in(key, 37)
    unit = jax.random.uniform(key, (SIZES, SIZES), jnp.float32, -1.0, 1.0)
    return dominant(unit, 0.1, 0.07).astype(jnp.bfloat16)


def steps_of(rng, dims, cuts, least, top_value):
    gain, own = 1.0, jax.random.fold_in(rng, 6)
    for position, blocks in cuts:
        draws = jnp.exp(jax.random.uniform(jax.random.fold_in(own, position), (blocks,), jnp.float32, least / len(cuts), top_value / len(cuts)))
        gain = gain * jnp.repeat(draws, dims[position] // blocks).reshape([-1 if axis == position else 1 for axis in range(len(dims))])
    return gain


def setup_inputs(seed: int = 0) -> dict:
    splits = jax.random.split(jax.random.key(seed), 13)
    return {
        "substrate": draw_substrate(jax.random.fold_in(splits[12], 71), 0),
        "oxygen": draw_oxygen(jax.random.fold_in(splits[12], 71), 0),
        "velocity": jnp.clip(jax.random.uniform(splits[2], (3, NZ, NX, NY), jnp.float32, -0.2, 0.2) * steps_of(splits[2], (3, NZ, NX, NY), ((1, 32), (2, 4), (3, 4)), -0.4, 0.0), -0.2, 0.2),
        "cell_map": draw_cell_map(jax.random.fold_in(splits[12], 71), 0),
        "owner_slot": draw_owner_slot(jax.random.fold_in(splits[12], 71), 0),
        "flow_list": draw_flow_list(jax.random.fold_in(splits[12], 71), 0),
        "flow_rates": jnp.clip(jnp.exp(jax.random.uniform(splits[6], (RATES,), jnp.float32, math.log(0.05), math.log(0.4))), 0.05, 0.4),
        "population": jnp.clip(jnp.exp(math.log(1.0) - 2.9957323 * jax.random.uniform(splits[7], (DEVICES * SLOTS, AGES, SIZES), jnp.float32) ** steps_of(splits[7], (DEVICES * SLOTS, AGES, SIZES), ((0, 512),), -0.2, 0.2)), 0.05, 1.0),
        "growth": draw_growth(jax.random.fold_in(splits[12], 71), 0),
        "daughter_kernel": draw_daughter_kernel(jax.random.fold_in(splits[12], 71), 0),
        "division_rate": jnp.clip(jnp.exp(jax.random.uniform(splits[10], (AGES, SIZES), jnp.float32, math.log(0.02), math.log(0.6))), 0.02, 0.6),
        "uptake_weight": jnp.clip(jnp.exp(jax.random.uniform(splits[11], (2, SIZES), jnp.float32, math.log(0.1), math.log(1.0))), 0.1, 1.0),
    }


diffusion = 0.05
growth_max = 0.8
half_substrate = 0.3
half_oxygen = 0.1
uptake_gain = 3.0


def stencil(padded, velocity):
    center = padded[:, 1:-1, 1:-1, 1:-1]
    lower_side = [padded[:, :-2, 1:-1, 1:-1], padded[:, 1:-1, :-2, 1:-1], padded[:, 1:-1, 1:-1, :-2]]
    upper_side = [padded[:, 2:, 1:-1, 1:-1], padded[:, 1:-1, 2:, 1:-1], padded[:, 1:-1, 1:-1, 2:]]
    total_change = center
    for axis_id in range(3):
        courant = velocity[axis_id][None]
        total_change = total_change + diffusion * (lower_side[axis_id] + upper_side[axis_id] - 2.0 * center)
        total_change = total_change - jnp.maximum(courant, 0.0) * (center - lower_side[axis_id])
        total_change = total_change - jnp.minimum(courant, 0.0) * (upper_side[axis_id] - center)
    return total_change


def grow(block_pop, rate_block, growth, daughter_kernel, division_rate):
    rate_scale = rate_block[:, None, None]
    growth_wide = growth.astype(jnp.float32)
    for substep in range(SUBSTEPS):
        low_pop = lax.optimization_barrier(block_pop.astype(jnp.bfloat16))
        moved_pop = jnp.einsum('mas,st->mat', low_pop.astype(jnp.float32), growth_wide, precision=lax.Precision.HIGHEST)
        grown_pop = block_pop + rate_scale * (moved_pop - block_pop)
        split_pop = division_rate[None] * rate_scale * grown_pop
        remain = grown_pop - split_pop
        mothers = jnp.sum(split_pop, axis=1).astype(jnp.bfloat16)
        newborn = 2.0 * jnp.dot(mothers, daughter_kernel, preferred_element_type=jnp.float32)
        oldest = remain[:, AGES - 2] + remain[:, AGES - 1]
        block_pop = jnp.concatenate([newborn[:, None], remain[:, :AGES - 2], oldest[:, None]], axis=1)
    return block_pop


def reference(substrate, oxygen, velocity, cell_map, owner_slot, flow_list, flow_rates, population, growth, daughter_kernel, division_rate, uptake_weight):
    fields = jnp.stack([substrate, oxygen])
    padded = jnp.pad(fields, ((0, 0), (1, 1), (1, 1), (1, 1)))
    swept_fields = stencil(padded, velocity)
    flat_map = cell_map.reshape(-1)
    field_sums = jnp.stack([jax.ops.segment_sum(swept_fields[index].reshape(-1), flat_map, num_segments=COMPS) for index in range(2)])
    means_all = field_sums / CELLS
    rate_all = growth_max * means_all[0] / (half_substrate + means_all[0]) * means_all[1] / (half_oxygen + means_all[1])
    owned_pop = population[owner_slot]
    biomass = jnp.einsum('kas,js->jk', owned_pop, uptake_weight, precision=lax.Precision.HIGHEST) / (AGES * SIZES)
    uptake = uptake_gain * rate_all[None] * biomass
    halves = jnp.array([half_substrate, half_oxygen], dtype=jnp.float32)[:, None, None, None]
    drawn_cells = uptake[:, cell_map]
    fields_out = swept_fields - drawn_cells * swept_fields / (halves + swept_fields)
    block_size = COMP_DEV * 32
    grouped = owned_pop.reshape(COMPS // block_size, block_size, AGES, SIZES)
    rate_groups = rate_all.reshape(COMPS // block_size, block_size)
    result = lax.map(lambda packed: grow(packed[0], packed[1], growth, daughter_kernel, division_rate), (grouped, rate_groups))
    result = result.reshape(COMPS, AGES, SIZES)
    outflow = flow_rates[flow_list[1]][:, None, None] * result
    inflow = jax.ops.segment_sum(outflow, flow_list[0], num_segments=COMPS)
    final_pop = result - outflow + inflow
    population_out = jnp.zeros_like(population).at[owner_slot].set(final_pop)
    return fields_out[0], fields_out[1], population_out
```

```python
import functools

import jax
import jax.numpy as jnp
from jax import lax
from jax.experimental import pallas as pl
from jax.experimental.pallas import tpu as pltpu
from jax.sharding import PartitionSpec as P

SUBSTEPS = 8
CELLS = 1024
SLOTS = 31
AGES = 64
SIZES = 256
COLS = 16
DEPTH = 32
LANES = 128
GROUP = 8
NONE_KEY = 65536.0

diffusion = 0.05
growth_max = 0.8
half_substrate = 0.3
half_oxygen = 0.1
uptake_gain = 3.0

MESH = pl.DeviceIdType.MESH
VMEM_SPEC = pl.BlockSpec(memory_space=pltpu.VMEM)
SMEM_SPEC = pl.BlockSpec(memory_space=pltpu.SMEM)
ANY_SPEC = pl.BlockSpec(memory_space=pl.ANY)
VMEM_BYTES = 48 * 1024 * 1024


def iota(shape, dim):
    return lax.broadcasted_iota(jnp.int32, shape, dim)


def device_of(slot):
    return (slot * 33826) >> 20


def lookup(table_row, index, high, row_id, total):
    row = jnp.broadcast_to(table_row, index.shape)
    found = jnp.take_along_axis(row, index, axis=1)
    return jnp.where(high == row_id, found, total)


def prepare_kernel(
    owner_ref,
    flow_ref,
    map_ref,
    weight_ref,
    pop_ref,
    pos_ref,
    bio_ref,
    list_ref,
    payload_ref,
    pop_vmem,
    target_ref,
    index_ref,
    place_ref,
    row_ref,
    ages_ref,
    list_smem,
    pop_sem,
    list_sem,
    pay_sem,
):
    column = lax.axis_index("gx") * 4 + lax.axis_index("gy")
    depth = lax.axis_index("gz")
    me = column * DEPTH + depth
    load = pltpu.make_async_copy(pop_ref, pop_vmem.at[pl.ds(0, SLOTS)], pop_sem)
    load.start()
    for row in range(64):
        lanes = slice(row * LANES, (row + 1) * LANES)
        target_ref[row : row + 1, :] = flow_ref[0:1, lanes]
        index_ref[row : row + 1, :] = flow_ref[1:2, lanes]

    owner = owner_ref[...]
    targets = target_ref[...]
    low, high = targets & 127, targets >> 7
    target_slot = jnp.zeros_like(owner)
    for row in range(64):
        target_slot = lookup(owner_ref[row : row + 1, :], low, high, row, target_slot)
    rate_index = index_ref[...]
    source_dev = device_of(owner)
    source_local = owner - source_dev * SLOTS
    target_dev = device_of(target_slot)
    target_local = target_slot - target_dev * SLOTS
    send_key = (source_local * 16 + rate_index).astype(jnp.float32)
    recv_key = (source_local * 512 + target_local * 16 + rate_index).astype(jnp.float32)
    send_col = jnp.where(source_dev == me, target_dev >> 5, -1)
    recv_col = jnp.where(target_dev == me, source_dev >> 5, -1)
    for col in range(COLS):
        for kind, (key, cols) in enumerate(((send_key, send_col), (recv_key, recv_col))):
            hit = cols == col
            low_row = jnp.min(jnp.where(hit, key, NONE_KEY), axis=0, keepdims=True)
            high_row = jnp.max(jnp.where(hit, key, -1.0), axis=0, keepdims=True)
            at = kind * 32 + col
            row_ref[at : at + 1, :] = low_row
            row_ref[at + 16 : at + 17, :] = high_row
    square = (64, LANES)
    rows = row_ref[...]
    is_low = (iota((64, 1), 0) & 16) == 0
    reduced = jnp.where(
        is_low, jnp.min(rows, axis=1, keepdims=True), jnp.max(rows, axis=1, keepdims=True)
    )
    diagonal = jnp.where(iota(square, 0) == iota(square, 1), reduced, 0.0)
    list_ref[...] = jnp.sum(diagonal, axis=0, keepdims=True).astype(jnp.int32)
    to_scalar = pltpu.make_async_copy(list_ref, list_smem, list_sem)
    to_scalar.start()
    owned = jnp.where(source_dev == me, 1.0, 0.0)
    held = jnp.sum(jnp.sum(owned, axis=0, keepdims=True), axis=1, keepdims=True)

    load.wait()
    to_scalar.wait()
    for col in range(COLS):
        lowest, highest = list_smem[0, col], list_smem[0, col + 16]
        first = jnp.where(highest >= 0, lowest >> 4, 0)
        second = jnp.where(highest >= 0, highest >> 4, 0)
        for rank, slot in enumerate((first, second)):
            pltpu.make_async_copy(
                pop_vmem.at[slot],
                payload_ref.at[col, pl.ds(rank * AGES, AGES)],
                pay_sem.at[col * 2 + rank],
            ).start()

    core = source_dev & 1
    place_ref[...] = (source_dev >> 1) * 32 + jnp.where(core == 1, 31 - source_local, source_local)
    cells = map_ref[...].reshape(LANES, LANES)
    low, high = cells & 127, cells >> 7

    def find(step, total):
        for part in range(8):
            row = step * 8 + part
            total = lookup(place_ref[pl.ds(row, 1), :], low, high, row, total)
        return total

    place = lax.fori_loop(0, 8, find, jnp.zeros_like(cells))
    pos_ref[...] = place.reshape(pos_ref.shape)

    for slot in range(SLOTS):
        ages_ref[slot : slot + 1, :] = jnp.sum(pop_vmem[slot], axis=0, keepdims=True)
    ages_ref[SLOTS : SLOTS + 1, :] = jnp.zeros((1, SIZES), jnp.float32)
    summed = ages_ref[...]
    block = (depth >> 1) & 3
    wide = (32, LANES)
    lane = iota(wide, 1)
    local = lane & 31
    slot_of_lane = jnp.where((depth & 1) == 1, 31 - local, local)
    here = ((lane >> 5) == block) & (slot_of_lane == iota(wide, 0))
    here = here & (slot_of_lane.astype(jnp.float32) < held)
    for field in range(2):
        weighted = summed * weight_ref[field : field + 1, :]
        mass = jnp.sum(weighted, axis=1, keepdims=True) / (AGES * SIZES)
        bio_ref[field : field + 1, :] = jnp.sum(
            jnp.where(here, mass, 0.0), axis=0, keepdims=True
        )
    bio_ref[2:3, :] = jnp.sum(jnp.where(here, 1.0, 0.0), axis=0, keepdims=True)
    bio_ref[3:8, :] = jnp.zeros((5, LANES), jnp.float32)

    for item in range(2 * COLS):
        pltpu.make_async_copy(
            pop_vmem.at[0],
            payload_ref.at[item // 2, pl.ds((item % 2) * AGES, AGES)],
            pay_sem.at[item],
        ).wait()


def prepare(owner, flow, cell_map, weight, population):
    return pl.pallas_call(
        prepare_kernel,
        out_shape=(
            jax.ShapeDtypeStruct(cell_map.shape, jnp.int32),
            jax.ShapeDtypeStruct((8, LANES), jnp.float32),
            jax.ShapeDtypeStruct((1, LANES), jnp.int32),
            jax.ShapeDtypeStruct((COLS, 2 * AGES, SIZES), jnp.float32),
        ),
        in_specs=[VMEM_SPEC, VMEM_SPEC, VMEM_SPEC, VMEM_SPEC, ANY_SPEC],
        out_specs=(VMEM_SPEC, VMEM_SPEC, VMEM_SPEC, ANY_SPEC),
        scratch_shapes=[
            pltpu.VMEM((32, AGES, SIZES), jnp.float32),
            pltpu.VMEM((64, LANES), jnp.int32),
            pltpu.VMEM((64, LANES), jnp.int32),
            pltpu.VMEM((64, LANES), jnp.int32),
            pltpu.VMEM((64, LANES), jnp.float32),
            pltpu.VMEM((32, SIZES), jnp.float32),
            pltpu.SMEM((1, LANES), jnp.int32),
            pltpu.SemaphoreType.DMA,
            pltpu.SemaphoreType.DMA,
            pltpu.SemaphoreType.DMA((2 * COLS,)),
        ],
        compiler_params=pltpu.CompilerParams(vmem_limit_bytes=VMEM_BYTES),
        cost_estimate=pl.CostEstimate(flops=8_000_000, bytes_accessed=6_000_000, transcendentals=0),
    )(owner, flow, cell_map, weight, population)


def sweep_kernel(
    sub_ref,
    oxy_ref,
    vel_ref,
    pos_ref,
    bio_ref,
    swept_ref,
    table_ref,
    x_send,
    x_recv,
    y_send,
    y_recv,
    z_recv,
    value_ref,
    sums_ref,
    a_recv,
    b_send,
    b_recv,
    c_send,
    c_recv,
    d_send,
    d_recv,
    halo_send_sem,
    halo_recv_sem,
    send_sem,
    recv_sem,
):
    gx, gy, gz = lax.axis_index("gx"), lax.axis_index("gy"), lax.axis_index("gz")
    column = gx * 4 + gy
    col_peers = [lax.rem(column + step, COLS) for step in range(1, COLS)]
    deep_peers = [lax.rem(gz + step, DEPTH) for step in range(1, DEPTH)]
    col_ids = [(peer // 4, lax.rem(peer, 4), gz) for peer in col_peers]
    deep_ids = [(gx, gy, peer) for peer in deep_peers]

    barrier = pltpu.get_barrier_semaphore()
    for peer in col_ids + deep_ids:
        pl.semaphore_signal(barrier, inc=1, device_id=peer, device_id_type=MESH)

    fields = (sub_ref, oxy_ref)
    for field, ref in enumerate(fields):
        layers = slice(field * 4, field * 4 + 4)
        x_send[0, layers, :] = ref[:, 0, :]
        x_send[1, layers, :] = ref[:, 31, :]
        turned = ref[...].reshape(LANES, LANES).T
        y_send[0, field : field + 1, :] = turned[0:1, :]
        y_send[1, field : field + 1, :] = turned[LANES - 1 : LANES, :]
    pl.semaphore_wait(barrier, len(col_ids) + len(deep_ids))

    halos = []
    for side in range(2):
        step = 3 if side == 0 else 1
        near_x = (lax.rem(gx + step, 4), gy, gz)
        near_y = (gx, lax.rem(gy + step, 4), gz)
        near_z = (gx, gy, lax.rem(gz + (DEPTH - 1 if side == 0 else 1), DEPTH))
        layer = 0 if side == 0 else 3
        pairs = [
            (x_send.at[side], x_recv.at[1 - side], near_x),
            (y_send.at[side], y_recv.at[1 - side], near_y),
            (sub_ref.at[layer], z_recv.at[1 - side, 0], near_z),
            (oxy_ref.at[layer], z_recv.at[1 - side, 1], near_z),
        ]
        for number, (source, target, device) in enumerate(pairs):
            sem = side * 4 + number
            halos.append(
                pltpu.make_async_remote_copy(
                    src_ref=source,
                    dst_ref=target,
                    send_sem=halo_send_sem.at[sem],
                    recv_sem=halo_recv_sem.at[sem],
                    device_id=device,
                    device_id_type=MESH,
                )
            )
    for copy in halos:
        copy.start()
    for copy in halos:
        copy.wait()

    shape = (4, 32, LANES)
    row_id = iota(shape, 1)
    lane_id = iota(shape, 2)
    inside = [
        (jnp.where(at > 0, 1.0, 0.0), jnp.where(at < count - 1, 1.0, 0.0))
        for at, count in ((gz, DEPTH), (gx, 4), (gy, 4))
    ]
    for field, ref in enumerate(fields):
        center = ref[...]
        layers = slice(field * 4, field * 4 + 4)
        z_low = (z_recv[0, field] * inside[0][0])[None]
        z_high = (z_recv[1, field] * inside[0][1])[None]
        x_low = (x_recv[0, layers, :] * inside[1][0])[:, None, :]
        x_high = (x_recv[1, layers, :] * inside[1][1])[:, None, :]
        y_edges = []
        for side in range(2):
            edge = y_recv[side, field : field + 1, :] * inside[2][side]
            y_edges.append(jnp.broadcast_to(edge, (LANES, LANES)).T.reshape(shape))
        lower = (
            jnp.concatenate([z_low, center[:3]], axis=0),
            jnp.where(row_id == 0, x_low, pltpu.roll(center, 1, 1)),
            jnp.where(lane_id == 0, y_edges[0], pltpu.roll(center, 1, 2)),
        )
        upper = (
            jnp.concatenate([center[1:], z_high], axis=0),
            jnp.where(row_id == 31, x_high, pltpu.roll(center, 31, 1)),
            jnp.where(lane_id == LANES - 1, y_edges[1], pltpu.roll(center, LANES - 1, 2)),
        )
        total = center
        for axis in range(3):
            courant = vel_ref[axis]
            total = total + diffusion * (lower[axis] + upper[axis] - 2.0 * center)
            total = total - jnp.maximum(courant, 0.0) * (center - lower[axis])
            total = total - jnp.minimum(courant, 0.0) * (upper[axis] - center)
        swept_ref[field] = total
        value_ref[field] = total.reshape(LANES, LANES)

    square = (LANES, LANES)
    sub_row = iota(square, 0)
    row_half = sub_row >> 1
    even = (sub_row & 1) == 0

    def gather_sums(step, total):
        rows = pl.ds(pl.multiple_of(step * 8, 8), 8)
        place = pos_ref[step // 4, pl.ds(pl.multiple_of(lax.rem(step, 4) * 8, 8), 8), :]
        first = value_ref[0, rows, :]
        second = value_ref[1, rows, :]
        left, right = [], []
        for row in range(8):
            one = slice(row, row + 1)
            value = jnp.where(even, first[one], second[one])
            coarse = value.astype(jnp.bfloat16).astype(jnp.float32)
            hit = (place[one] >> 7) == row_half
            top = jnp.where(hit, coarse, 0.0).astype(jnp.bfloat16)
            rest = jnp.where(hit, value - coarse, 0.0).astype(jnp.bfloat16)
            left.append(jnp.concatenate([top, rest], axis=0))
            right.append(jnp.where((place[one] & 127) == sub_row, 1.0, 0.0).astype(jnp.bfloat16))
        return total + lax.dot_general(
            jnp.concatenate(left, axis=1),
            jnp.concatenate(right, axis=1),
            (((1,), (1,)), ((), ())),
            preferred_element_type=jnp.float32,
        )

    sums = lax.fori_loop(0, 16, gather_sums, jnp.zeros((2 * LANES, LANES), jnp.float32))
    sums_ref[...] = (sums[:LANES] + sums[LANES:]).reshape(COLS, 8, LANES)

    def exchange(stage, ids, source_of, target):
        copies = []
        for number, device in enumerate(ids):
            copies.append(
                pltpu.make_async_remote_copy(
                    src_ref=source_of(number),
                    dst_ref=target,
                    send_sem=send_sem.at[stage],
                    recv_sem=recv_sem.at[stage],
                    device_id=device,
                    device_id_type=MESH,
                )
            )
        for copy in copies:
            copy.start()

    def arrived(stage, buffer, count):
        part = buffer.at[pl.ds(0, count)]
        pltpu.make_async_copy(part, part, recv_sem.at[stage]).wait()

    def left_here(stage, buffer, count):
        part = buffer.at[pl.ds(0, count)]
        pltpu.make_async_copy(part, part, send_sem.at[stage]).wait()

    exchange(0, col_ids, lambda number: sums_ref.at[col_peers[number]], a_recv.at[column])
    a_recv[column] = sums_ref[column]
    arrived(0, a_recv, COLS - 1)
    part = jnp.sum(a_recv[...], axis=0)
    for block in range(4):
        b_send[block] = part[2 * block : 2 * block + 2, :]
    exchange(1, deep_ids, lambda number: b_send.at[deep_peers[number] // 8], b_recv.at[gz])
    b_recv[gz] = b_send[gz // 8]
    arrived(1, b_recv, DEPTH - 1)
    means = jnp.sum(b_recv[...], axis=0) / CELLS
    mean_sub, mean_oxy = means[0:1, :], means[1:2, :]
    rate = growth_max * mean_sub / (half_substrate + mean_sub) * mean_oxy / (half_oxygen + mean_oxy)
    packed = uptake_gain * rate * bio_ref[0:1, :]
    packed = packed + pltpu.roll(uptake_gain * rate * bio_ref[1:2, :], 32, 1)
    packed = packed + pltpu.roll(rate * bio_ref[2:3, :], 64, 1)

    c_send[0] = packed
    exchange(2, deep_ids, lambda number: c_send.at[0], c_recv.at[gz])
    c_recv[gz] = packed
    arrived(2, c_recv, DEPTH - 1)
    rows = c_recv[...].reshape(DEPTH, LANES)
    wide = (DEPTH, LANES)
    mine = (iota(wide, 1) >> 5) == ((iota(wide, 0) >> 1) & 3)
    for item in range(3):
        turned = rows if item == 0 else pltpu.roll(rows, LANES - 32 * item, 1)
        kept = jnp.where(mine, turned, 0.0)
        for block in range(4):
            at = item * 4 + block
            d_send[0, at : at + 1, :] = jnp.sum(
                kept[8 * block : 8 * block + 8, :], axis=0, keepdims=True
            )
    d_send[0, 12:16, :] = jnp.zeros((4, LANES), jnp.float32)
    exchange(3, col_ids, lambda number: d_send.at[0], d_recv.at[column])
    d_recv[column] = d_send[0]
    arrived(3, d_recv, COLS - 1)
    table_ref[...] = d_recv[...]

    left_here(0, a_recv, COLS - 1)
    left_here(1, b_recv, DEPTH - 1)
    left_here(2, c_recv, DEPTH - 1)
    left_here(3, d_recv, COLS - 1)


def sweep(substrate, oxygen, velocity, pos, bio):
    f32 = jnp.float32
    return pl.pallas_call(
        sweep_kernel,
        out_shape=(
            jax.ShapeDtypeStruct((2,) + substrate.shape, f32),
            jax.ShapeDtypeStruct((COLS, 16, LANES), f32),
        ),
        in_specs=[VMEM_SPEC] * 5,
        out_specs=(VMEM_SPEC, VMEM_SPEC),
        scratch_shapes=[
            pltpu.VMEM((2, 8, LANES), f32),
            pltpu.VMEM((2, 8, LANES), f32),
            pltpu.VMEM((2, 2, LANES), f32),
            pltpu.VMEM((2, 2, LANES), f32),
            pltpu.VMEM((2, 2, 32, LANES), f32),
            pltpu.VMEM((2, LANES, LANES), f32),
            pltpu.VMEM((COLS, 8, LANES), f32),
            pltpu.VMEM((COLS, 8, LANES), f32),
            pltpu.VMEM((4, 2, LANES), f32),
            pltpu.VMEM((DEPTH, 2, LANES), f32),
            pltpu.VMEM((1, 1, LANES), f32),
            pltpu.VMEM((DEPTH, 1, LANES), f32),
            pltpu.VMEM((1, 16, LANES), f32),
            pltpu.VMEM((COLS, 16, LANES), f32),
            pltpu.SemaphoreType.DMA((8,)),
            pltpu.SemaphoreType.DMA((8,)),
            pltpu.SemaphoreType.DMA((4,)),
            pltpu.SemaphoreType.DMA((4,)),
        ],
        compiler_params=pltpu.CompilerParams(
            collective_id=0, has_side_effects=True, vmem_limit_bytes=VMEM_BYTES
        ),
        cost_estimate=pl.CostEstimate(
            flops=1_200_000_000, bytes_accessed=1_000_000, transcendentals=0
        ),
    )(substrate, oxygen, velocity, pos, bio)


def grow_kernel(
    swept_ref,
    pos_ref,
    table_ref,
    list_ref,
    flow_rate_ref,
    growth_ref,
    daughter_ref,
    division_ref,
    pop_ref,
    incoming_ref,
    sub_out_ref,
    oxy_out_ref,
    pop_out_ref,
    state,
    mother_ref,
    rate_rows,
    rate_table,
    rate_of,
    scale_of,
    target_of,
    state_sem,
    table_sem,
):
    depth = lax.axis_index("gz")
    core = depth & 1
    block = (depth >> 1) & 3
    quarter = depth >> 3
    own_column = lax.axis_index("gx") * 4 + lax.axis_index("gy")

    rows = jnp.zeros((COLS, LANES), jnp.float32)
    for part in range(4):
        rows = rows + jnp.where(quarter == part, table_ref[:, 8 + part, :], 0.0)
    rate_rows[...] = rows
    to_scalar = pltpu.make_async_copy(rate_rows, rate_table, table_sem)
    to_scalar.start()

    own = jnp.int32(0)
    for col in range(COLS):
        lowest, highest = list_ref[0, col], list_ref[0, col + 16]
        own = own + jnp.where(highest >= 0, 1, 0) + jnp.where(highest > lowest, 1, 0)

    def fetch_own(slot, carry):
        pltpu.make_async_copy(pop_ref.at[slot], state.at[slot], state_sem.at[0]).start()
        return carry

    lax.fori_loop(0, own, fetch_own, 0)
    to_scalar.wait()

    def lane_of(slot):
        return block * 32 + jnp.where(core == 1, 31 - slot, slot)

    def own_rate(slot, carry):
        rate_of[slot] = rate_table[own_column, lane_of(slot)]
        return carry

    lax.fori_loop(0, own, own_rate, 0)

    def scan_own(col, carry):
        lowest, highest = list_ref[0, col], list_ref[0, col + 16]

        @pl.when(highest >= 0)
        def _():
            scale_of[lowest >> 4] = flow_rate_ref[lowest & 15]
            scale_of[highest >> 4] = flow_rate_ref[highest & 15]

        return carry

    lax.fori_loop(0, COLS, scan_own, 0)

    def scan_arriving(item, count):
        col, rank = item >> 1, item & 1
        lowest, highest = list_ref[0, col + 32], list_ref[0, col + 48]
        key = jnp.where(rank == 0, lowest, highest)
        valid = jnp.where(rank == 0, highest >= 0, highest > lowest)

        @pl.when(valid)
        def _():
            rate_of[count] = rate_table[col, lane_of(key >> 9)]
            scale_of[count] = flow_rate_ref[key & 15]
            target_of[count] = (key >> 4) & 31
            pltpu.make_async_copy(
                incoming_ref.at[col, pl.ds(pl.multiple_of(rank * AGES, AGES), AGES)],
                state.at[count],
                state_sem.at[0],
            ).start()

        return count + jnp.where(valid, 1, 0)

    total = lax.fori_loop(0, 2 * COLS, scan_arriving, own)

    cells = pos_ref[...].reshape(LANES, LANES)
    low, high = cells & 127, cells >> 7

    def find(col, drawn):
        first, second = drawn
        tile = table_ref[col]
        for part in range(4):
            row = col * 4 + part
            first = lookup(tile[part : part + 1, :], low, high, row, first)
            second = lookup(tile[4 + part : 5 + part, :], low, high, row, second)
        return first, second

    zero = jnp.zeros((LANES, LANES), jnp.float32)
    drawn = lax.fori_loop(0, COLS, find, (zero, zero))
    for field, (out, half) in enumerate(
        ((sub_out_ref, half_substrate), (oxy_out_ref, half_oxygen))
    ):
        swept = swept_ref[field]
        out[...] = swept - drawn[field].reshape(swept.shape) * swept / (half + swept)

    def fetched(slot, carry):
        pltpu.make_async_copy(pop_ref.at[0], state.at[slot], state_sem.at[0]).wait()
        return carry

    lax.fori_loop(0, total, fetched, 0)

    groups = (total + GROUP - 1) // GROUP
    for step in range(SUBSTEPS):
        oldest = AGES - 1 - step
        turn = step

        def one_group(group, carry, oldest=oldest, turn=turn):
            base = group * GROUP
            held = state[pl.ds(base, GROUP)]
            moved = jnp.dot(
                held.reshape(GROUP * AGES, SIZES).astype(jnp.bfloat16),
                growth_ref[...],
                preferred_element_type=jnp.float32,
            ).reshape(GROUP, AGES, SIZES)
            for slot in range(GROUP):
                rate = rate_of[base + slot]
                grown = held[slot] + rate * (moved[slot] - held[slot])
                divided = (division_ref[turn] * rate) * grown
                remain = grown - divided
                mother_ref[pl.ds(base + slot, 1), :] = jnp.sum(divided, axis=0, keepdims=True)
                state[base + slot] = remain
                state[base + slot, oldest - 1 : oldest, :] = (
                    remain[oldest - 1 : oldest, :] + remain[oldest : oldest + 1, :]
                )
            return carry

        lax.fori_loop(0, groups, one_group, 0)
        newborn = 2.0 * jnp.dot(
            mother_ref[...].astype(jnp.bfloat16),
            daughter_ref[...],
            preferred_element_type=jnp.float32,
        )
        state[:, oldest, :] = newborn

    top = AGES - SUBSTEPS
    for slot in range(SLOTS):

        @pl.when(slot < own)
        def _():
            kept = state[slot]
            kept = kept - scale_of[slot] * kept
            pop_out_ref[slot, :SUBSTEPS, :] = kept[top:]
            pop_out_ref[slot, SUBSTEPS:, :] = kept[:top]

        @pl.when(slot >= own)
        def _():
            pop_out_ref[slot] = jnp.zeros((AGES, SIZES), jnp.float32)

    def arrive(item, carry):
        slot = target_of[item]
        inflow = scale_of[item] * state[item]
        pop_out_ref[slot, :SUBSTEPS, :] = pop_out_ref[slot, :SUBSTEPS, :] + inflow[top:]
        pop_out_ref[slot, SUBSTEPS:, :] = pop_out_ref[slot, SUBSTEPS:, :] + inflow[:top]
        return carry

    lax.fori_loop(own, total, arrive, 0)


def grow(swept, pos, table, lists, flow_rates, growth, daughter, division, population, incoming):
    f32 = jnp.float32
    field = jax.ShapeDtypeStruct(pos.shape, f32)
    turned = jnp.stack([jnp.roll(division, -step, axis=0) for step in range(SUBSTEPS)])
    return pl.pallas_call(
        grow_kernel,
        out_shape=(field, field, jax.ShapeDtypeStruct(population.shape, f32)),
        in_specs=[VMEM_SPEC] * 3
        + [SMEM_SPEC] * 2
        + [VMEM_SPEC] * 3
        + [ANY_SPEC] * 2,
        out_specs=(VMEM_SPEC,) * 3,
        scratch_shapes=[
            pltpu.VMEM((64, AGES, SIZES), f32),
            pltpu.VMEM((64, SIZES), f32),
            pltpu.VMEM((COLS, LANES), f32),
            pltpu.SMEM((COLS, LANES), f32),
            pltpu.SMEM((64,), f32),
            pltpu.SMEM((64,), f32),
            pltpu.SMEM((64,), jnp.int32),
            pltpu.SemaphoreType.DMA((1,)),
            pltpu.SemaphoreType.DMA,
        ],
        compiler_params=pltpu.CompilerParams(vmem_limit_bytes=VMEM_BYTES),
        cost_estimate=pl.CostEstimate(
            flops=3_000_000_000, bytes_accessed=8_000_000, transcendentals=0
        ),
    )(swept, pos, table, lists, flow_rates, growth, daughter, turned, population, incoming)


def per_device(
    substrate,
    oxygen,
    velocity,
    cell_map,
    owner_slot,
    flow_list,
    flow_rates,
    population,
    growth,
    daughter_kernel,
    division_rate,
    uptake_weight,
):
    pos, bio, lists, payload = prepare(
        owner_slot.reshape(64, LANES), flow_list, cell_map, uptake_weight, population
    )
    incoming = lax.all_to_all(payload, ("gx", "gy"), split_axis=0, concat_axis=0, tiled=True)
    swept, table = sweep(substrate, oxygen, velocity, pos, bio)
    return grow(
        swept,
        pos,
        table,
        lists,
        flow_rates,
        growth,
        daughter_kernel,
        division_rate,
        population,
        incoming,
    )


def solution(mesh):
    return jax.shard_map(
        per_device,
        mesh=mesh,
        in_specs=(
            P("gz", "gx", "gy"),
            P("gz", "gx", "gy"),
            P(None, "gz", "gx", "gy"),
            P("gz", "gx", "gy"),
            P(),
            P(),
            P(),
            P(("gx", "gy", "gz"), None, None),
            P(),
            P(),
            P(),
            P(),
        ),
        out_specs=(P("gz", "gx", "gy"), P("gz", "gx", "gy"), P(("gx", "gy", "gz"), None, None)),
        check_vma=False,
    )
```

```python
import functools

import jax
import jax.numpy as jnp
from jax import lax
from jax.experimental import pallas as pl
from jax.experimental.pallas import tpu as pltpu
from jax.sharding import PartitionSpec as P

SUBSTEPS = 8
CELLS = 1024
SLOTS = 31
AGES = 64
SIZES = 256
COLS = 16
DEPTH = 32
LANES = 128
GROUP = 8
NONE_KEY = 65536.0

diffusion = 0.05
growth_max = 0.8
half_substrate = 0.3
half_oxygen = 0.1
uptake_gain = 3.0

FLOW_PARTS = (
    ((1, 0), (3, 0), (0, 1), (0, 3)),
    ((2, 0), (0, 2), (1, 1), (3, 3), (1, 3), (3, 1)),
    ((1, 2), (2, 1), (2, 3), (3, 2), (2, 2)),
)

MESH = pl.DeviceIdType.MESH
VMEM_SPEC = pl.BlockSpec(memory_space=pltpu.VMEM)
SMEM_SPEC = pl.BlockSpec(memory_space=pltpu.SMEM)
HBM_SPEC = pl.BlockSpec(memory_space=pltpu.HBM)
VMEM_BYTES = 48 * 1024 * 1024


def iota(shape, dim):
    return lax.broadcasted_iota(jnp.int32, shape, dim)


def device_of(slot):
    return (slot * 33826) >> 20


def lookup(table_row, index, high, row_id, total):
    row = jnp.broadcast_to(table_row, index.shape)
    found = jnp.take_along_axis(row, index, axis=1, mode="promise_in_bounds")
    return jnp.where(high == row_id, found, total)


def prepare_kernel(
    owner_hbm,
    flow_hbm,
    pop_ref,
    list_ref,
    payload_ref,
    owner_ref,
    flow_ref,
    target_ref,
    index_ref,
    row_ref,
    list_smem,
    load_sem,
    list_sem,
    pay_sem,
):
    column = lax.axis_index("gx") * 4 + lax.axis_index("gy")
    me = column * DEPTH + lax.axis_index("gz")
    loads = [
        pltpu.make_async_copy(owner_hbm, owner_ref, load_sem.at[0]),
        pltpu.make_async_copy(flow_hbm, flow_ref, load_sem.at[1]),
    ]
    for load in loads:
        load.start()
    for load in loads:
        load.wait()
    for row in range(64):
        lanes = slice(row * LANES, (row + 1) * LANES)
        target_ref[row : row + 1, :] = flow_ref[0:1, lanes]
        index_ref[row : row + 1, :] = flow_ref[1:2, lanes]

    owner = owner_ref[...]
    targets = target_ref[...]
    low, high = targets & 127, targets >> 7
    target_slot = jnp.zeros_like(owner)
    for row in range(64):
        target_slot = lookup(owner_ref[row : row + 1, :], low, high, row, target_slot)
    rate_index = index_ref[...]
    source_dev = device_of(owner)
    source_local = owner - source_dev * SLOTS
    target_dev = device_of(target_slot)
    target_local = target_slot - target_dev * SLOTS
    send_key = (source_local * 16 + rate_index).astype(jnp.float32)
    recv_key = (source_local * 512 + target_local * 16 + rate_index).astype(jnp.float32)
    send_col = jnp.where(source_dev == me, target_dev >> 5, -1)
    recv_col = jnp.where(target_dev == me, source_dev >> 5, -1)
    for col in range(COLS):
        for kind, (key, cols) in enumerate(((send_key, send_col), (recv_key, recv_col))):
            hit = cols == col
            low_row = jnp.min(jnp.where(hit, key, NONE_KEY), axis=0, keepdims=True)
            high_row = jnp.max(jnp.where(hit, key, -1.0), axis=0, keepdims=True)
            at = kind * 32 + col
            row_ref[at : at + 1, :] = low_row
            row_ref[at + 16 : at + 17, :] = high_row
    square = (64, LANES)
    rows = row_ref[...]
    is_low = (iota((64, 1), 0) & 16) == 0
    reduced = jnp.where(
        is_low, jnp.min(rows, axis=1, keepdims=True), jnp.max(rows, axis=1, keepdims=True)
    )
    diagonal = jnp.where(iota(square, 0) == iota(square, 1), reduced, 0.0)
    list_ref[...] = jnp.sum(diagonal, axis=0, keepdims=True).astype(jnp.int32)
    to_scalar = pltpu.make_async_copy(list_ref, list_smem, list_sem)
    to_scalar.start()
    to_scalar.wait()
    for col in range(COLS):
        lowest, highest = list_smem[0, col], list_smem[0, col + 16]
        first = jnp.where(highest >= 0, lowest >> 4, 0)
        second = jnp.where(highest >= 0, highest >> 4, 0)
        for rank, slot in enumerate((first, second)):
            pltpu.make_async_copy(
                pop_ref.at[slot],
                payload_ref.at[col, pl.ds(rank * AGES, AGES)],
                pay_sem.at[col * 2 + rank],
            ).start()
    for item in range(2 * COLS):
        pltpu.make_async_copy(
            pop_ref.at[0],
            payload_ref.at[item // 2, pl.ds((item % 2) * AGES, AGES)],
            pay_sem.at[item],
        ).wait()


def prepare(owner, flow, population):
    return pl.pallas_call(
        prepare_kernel,
        out_shape=(
            jax.ShapeDtypeStruct((1, LANES), jnp.int32),
            jax.ShapeDtypeStruct((COLS, 2 * AGES, SIZES), jnp.float32),
        ),
        in_specs=[HBM_SPEC, HBM_SPEC, HBM_SPEC],
        out_specs=(VMEM_SPEC, HBM_SPEC),
        scratch_shapes=[
            pltpu.VMEM((64, LANES), jnp.int32),
            pltpu.VMEM(flow.shape, jnp.int32),
            pltpu.VMEM((64, LANES), jnp.int32),
            pltpu.VMEM((64, LANES), jnp.int32),
            pltpu.VMEM((64, LANES), jnp.float32),
            pltpu.SMEM((1, LANES), jnp.int32),
            pltpu.SemaphoreType.DMA((2,)),
            pltpu.SemaphoreType.DMA,
            pltpu.SemaphoreType.DMA((2 * COLS,)),
        ],
        compiler_params=pltpu.CompilerParams(vmem_limit_bytes=16 * 1024 * 1024),
        cost_estimate=pl.CostEstimate(flops=8_000_000, bytes_accessed=6_000_000, transcendentals=0),
    )(owner, flow, population)


def grow_rounds(state, rate_of, mother_ref, turned_ref, growth_ref, daughter_ref, groups):
    for step in range(SUBSTEPS):
        oldest = AGES - 1 - step

        def one_group(group, carry, oldest=oldest, step=step):
            base = group * GROUP
            held = state[pl.ds(base, GROUP)]
            moved = jnp.dot(
                held.reshape(GROUP * AGES, SIZES).astype(jnp.bfloat16),
                growth_ref[...],
                preferred_element_type=jnp.float32,
            ).reshape(GROUP, AGES, SIZES)
            for slot in range(GROUP):
                rate = rate_of(base + slot)
                grown = held[slot] + rate * (moved[slot] - held[slot])
                divided = (turned_ref[step] * rate) * grown
                remain = grown - divided
                mother_ref[pl.ds(base + slot, 1), :] = jnp.sum(divided, axis=0, keepdims=True)
                state[base + slot] = remain
                state[base + slot, oldest - 1 : oldest, :] = (
                    remain[oldest - 1 : oldest, :] + remain[oldest : oldest + 1, :]
                )
            return carry

        lax.fori_loop(0, groups, one_group, 0)
        newborn = 2.0 * jnp.dot(
            mother_ref[...].astype(jnp.bfloat16),
            daughter_ref[...],
            preferred_element_type=jnp.float32,
        )
        state[:, oldest, :] = newborn


def sweep_kernel(
    sub_ref,
    oxy_ref,
    vel_ref,
    map_ref,
    owner_ref,
    weight_ref,
    growth_ref,
    daughter_ref,
    division_ref,
    pop_ref,
    payload_ref,
    swept_ref,
    pos_ref,
    table_ref,
    turned_ref,
    state_ref,
    incoming_ref,
    x_send,
    x_recv,
    y_send,
    y_recv,
    z_recv,
    place_ref,
    ages_ref,
    mother_ref,
    value_ref,
    sums_ref,
    a_recv,
    pair_send,
    pair_recv,
    deep_send,
    deep_recv,
    bio_send,
    bio_recv,
    d_send,
    d_recv,
    rate_row,
    rate_smem,
    local_sem,
    halo_send_sem,
    halo_recv_sem,
    flow_send_sem,
    flow_recv_sem,
    send_sem,
    recv_sem,
):
    gx, gy, gz = lax.axis_index("gx"), lax.axis_index("gy"), lax.axis_index("gz")
    column = gx * 4 + gy
    chip, core = gz // 2, lax.rem(gz, 2)
    col_peers = [lax.rem(column + step, COLS) for step in range(1, COLS)]
    col_ids = [(peer // 4, lax.rem(peer, 4), gz) for peer in col_peers]
    deep_ids = [(gx, gy, lax.rem(gz + step, DEPTH)) for step in range(1, DEPTH)]
    same_core_ids = [(gx, gy, lax.rem(gz + step, DEPTH)) for step in range(2, DEPTH, 2)]
    sibling = (gx, gy, gz + 1 - 2 * core)

    barrier = pltpu.get_barrier_semaphore()
    for peer in col_ids + deep_ids:
        pl.semaphore_signal(barrier, inc=1, device_id=peer, device_id_type=MESH)
    load = pltpu.make_async_copy(pop_ref, state_ref.at[pl.ds(0, SLOTS)], local_sem.at[0])
    load.start()
    stay = pltpu.make_async_copy(
        payload_ref.at[column], incoming_ref.at[column], local_sem.at[1]
    )
    stay.start()

    def send(stage, ids, source_of, target):
        for number, device in enumerate(ids):
            pltpu.make_async_remote_copy(
                src_ref=source_of(number),
                dst_ref=target,
                send_sem=send_sem.at[stage],
                recv_sem=recv_sem.at[stage],
                device_id=device,
                device_id_type=MESH,
            ).start()

    def arrived(stage, buffer, count):
        part = buffer.at[pl.ds(0, count)]
        pltpu.make_async_copy(part, part, recv_sem.at[stage]).wait()

    def left_here(stage, buffer, count):
        part = buffer.at[pl.ds(0, count)]
        pltpu.make_async_copy(part, part, send_sem.at[stage]).wait()

    flows = []

    def send_flows(part):
        for step_x, step_y in FLOW_PARTS[part]:
            near_x, near_y = lax.rem(gx + step_x, 4), lax.rem(gy + step_y, 4)
            number = len(flows)
            copy = pltpu.make_async_remote_copy(
                src_ref=payload_ref.at[near_x * 4 + near_y],
                dst_ref=incoming_ref.at[column],
                send_sem=flow_send_sem.at[number],
                recv_sem=flow_recv_sem.at[number],
                device_id=(near_x, near_y, gz),
                device_id_type=MESH,
            )
            copy.start()
            flows.append(copy)

    fields = (sub_ref, oxy_ref)
    for field, ref in enumerate(fields):
        layers = slice(field * 4, field * 4 + 4)
        x_send[0, layers, :] = ref[:, 0, :]
        x_send[1, layers, :] = ref[:, 31, :]
        turned = ref[...].reshape(LANES, LANES).T
        y_send[0, field : field + 1, :] = turned[0:1, :]
        y_send[1, field : field + 1, :] = turned[LANES - 1 : LANES, :]

    owner = owner_ref[...]
    owner_dev = device_of(owner)
    owner_local = owner - owner_dev * SLOTS
    place_ref[...] = (owner_dev >> 1) * 32 + jnp.where(
        (owner_dev & 1) == 1, 31 - owner_local, owner_local
    )
    cells = map_ref[...].reshape(LANES, LANES)
    low, high = cells & 127, cells >> 7

    def find(step, total):
        for part in range(8):
            row = step * 8 + part
            total = lookup(place_ref[pl.ds(row, 1), :], low, high, row, total)
        return total

    place = lax.fori_loop(0, 8, find, jnp.zeros_like(cells))
    pos_ref[...] = place.reshape(pos_ref.shape)

    division = division_ref[...]
    turned_ref[0] = division
    for step in range(1, SUBSTEPS):
        turned_ref[step] = pltpu.roll(division, AGES - step, 0)

    load.wait()
    state_ref[SLOTS] = jnp.zeros((AGES, SIZES), jnp.float32)
    for slot in range(SLOTS + 1):
        ages_ref[slot : slot + 1, :] = jnp.sum(state_ref[slot], axis=0, keepdims=True)
    summed = ages_ref[...]
    owned = jnp.where(owner_dev == column * DEPTH + gz, 1.0, 0.0)
    held = jnp.sum(jnp.sum(owned, axis=0, keepdims=True), axis=1, keepdims=True)
    block = lax.rem(chip, 4)
    wide = (DEPTH, LANES)
    lane = iota(wide, 1)
    local = lane & 31
    slot_of_lane = jnp.where(core == 1, 31 - local, local)
    here = ((lane >> 5) == block) & (slot_of_lane == iota(wide, 0))
    here = here & (slot_of_lane.astype(jnp.float32) < held)
    masses = []
    for field in range(2):
        weighted = summed * weight_ref[field : field + 1, :]
        mass = jnp.sum(weighted, axis=1, keepdims=True) / (AGES * SIZES)
        masses.append(jnp.sum(jnp.where(here, mass, 0.0), axis=0, keepdims=True))
    packed = masses[0] + pltpu.roll(masses[1], 32, 1)
    bio_send[0] = packed
    bio_recv[gz] = packed

    pl.semaphore_wait(barrier, len(col_ids) + len(deep_ids))

    halos = []
    for side in range(2):
        step = 3 if side == 0 else 1
        near_x = (lax.rem(gx + step, 4), gy, gz)
        near_y = (gx, lax.rem(gy + step, 4), gz)
        near_z = (gx, gy, lax.rem(gz + (DEPTH - 1 if side == 0 else 1), DEPTH))
        layer = 0 if side == 0 else 3
        pairs = [
            (x_send.at[side], x_recv.at[1 - side], near_x),
            (y_send.at[side], y_recv.at[1 - side], near_y),
            (sub_ref.at[layer], z_recv.at[1 - side, 0], near_z),
            (oxy_ref.at[layer], z_recv.at[1 - side, 1], near_z),
        ]
        for number, (source, target, device) in enumerate(pairs):
            sem = side * 4 + number
            halos.append(
                pltpu.make_async_remote_copy(
                    src_ref=source,
                    dst_ref=target,
                    send_sem=halo_send_sem.at[sem],
                    recv_sem=halo_recv_sem.at[sem],
                    device_id=device,
                    device_id_type=MESH,
                )
            )
    for copy in halos:
        copy.start()
    send(0, deep_ids, lambda number: bio_send.at[0], bio_recv.at[gz])
    for copy in halos:
        copy.wait()
    send_flows(0)

    shape = (4, 32, LANES)
    row_id = iota(shape, 1)
    lane_id = iota(shape, 2)
    inside = [
        (jnp.where(at > 0, 1.0, 0.0), jnp.where(at < count - 1, 1.0, 0.0))
        for at, count in ((gz, DEPTH), (gx, 4), (gy, 4))
    ]
    for field, ref in enumerate(fields):
        center = ref[...]
        layers = slice(field * 4, field * 4 + 4)
        z_low = (z_recv[0, field] * inside[0][0])[None]
        z_high = (z_recv[1, field] * inside[0][1])[None]
        x_low = (x_recv[0, layers, :] * inside[1][0])[:, None, :]
        x_high = (x_recv[1, layers, :] * inside[1][1])[:, None, :]
        y_edges = []
        for side in range(2):
            edge = y_recv[side, field : field + 1, :] * inside[2][side]
            y_edges.append(jnp.broadcast_to(edge, (LANES, LANES)).T.reshape(shape))
        lower = (
            jnp.concatenate([z_low, center[:3]], axis=0),
            jnp.where(row_id == 0, x_low, pltpu.roll(center, 1, 1)),
            jnp.where(lane_id == 0, y_edges[0], pltpu.roll(center, 1, 2)),
        )
        upper = (
            jnp.concatenate([center[1:], z_high], axis=0),
            jnp.where(row_id == 31, x_high, pltpu.roll(center, 31, 1)),
            jnp.where(lane_id == LANES - 1, y_edges[1], pltpu.roll(center, LANES - 1, 2)),
        )
        total = center
        for axis in range(3):
            courant = vel_ref[axis]
            total = total + diffusion * (lower[axis] + upper[axis] - 2.0 * center)
            total = total - jnp.maximum(courant, 0.0) * (center - lower[axis])
            total = total - jnp.minimum(courant, 0.0) * (upper[axis] - center)
        swept_ref[field] = total
        value_ref[field] = total.reshape(LANES, LANES)

    fine_row = iota((2 * LANES, LANES), 0)
    sub_row = iota((64, LANES), 0)
    row_half = sub_row >> 1
    even = (sub_row & 1) == 0

    def gather_sums(step, total):
        rows = pl.ds(pl.multiple_of(step * 8, 8), 8)
        place = pos_ref[step // 4, pl.ds(pl.multiple_of(lax.rem(step, 4) * 8, 8), 8), :]
        first = value_ref[0, rows, :]
        second = value_ref[1, rows, :]
        left, right = [], []
        for row in range(8):
            one = slice(row, row + 1)
            value = jnp.where(even, first[one], second[one])
            coarse = value.astype(jnp.bfloat16).astype(jnp.float32)
            hit = (place[one] >> 8) == row_half
            top = jnp.where(hit, coarse, 0.0).astype(jnp.bfloat16)
            rest = jnp.where(hit, value - coarse, 0.0).astype(jnp.bfloat16)
            left.append(jnp.concatenate([top, rest], axis=0))
            right.append(jnp.where((place[one] & 255) == fine_row, 1.0, 0.0).astype(jnp.bfloat16))
        return total + lax.dot_general(
            jnp.concatenate(left, axis=1),
            jnp.concatenate(right, axis=1),
            (((1,), (1,)), ((), ())),
            preferred_element_type=jnp.float32,
        )

    sums = lax.fori_loop(0, 16, gather_sums, jnp.zeros((LANES, 2 * LANES), jnp.float32))
    sums_ref[...] = (sums[:64] + sums[64:]).reshape(COLS, 4, 2 * LANES)

    send(1, col_ids, lambda number: sums_ref.at[col_peers[number]], a_recv.at[column])
    a_recv[column] = sums_ref[column]
    arrived(1, a_recv, COLS - 1)
    send_flows(1)
    part = jnp.sum(a_recv[...], axis=0)
    split = []
    for field in range(2):
        split.append(
            jnp.concatenate(
                [
                    part[2 * (row // 2) + field : 2 * (row // 2) + field + 1][
                        :, (row % 2) * LANES : (row % 2 + 1) * LANES
                    ]
                    for row in range(4)
                ],
                axis=0,
            )
        )

    first_core = core == 0
    pair_send[0] = jnp.where(first_core, split[1], split[0])
    send(2, [sibling], lambda number: pair_send.at[0], pair_recv.at[0])
    arrived(2, pair_recv, 1)
    chip_sum = jnp.where(first_core, split[0], split[1]) + pair_recv[0]
    deep_send[0] = chip_sum
    send(3, same_core_ids, lambda number: deep_send.at[0], deep_recv.at[chip])
    deep_recv[chip] = chip_sum
    arrived(3, deep_recv, 15)
    added = jnp.sum(deep_recv[...], axis=0)
    pair_send[1] = added
    send(4, [sibling], lambda number: pair_send.at[1], pair_recv.at[1])
    arrived(4, pair_recv, 1)
    other = pair_recv[1]
    mean_sub = jnp.where(first_core, added, other) / CELLS
    mean_oxy = jnp.where(first_core, other, added) / CELLS
    rate = growth_max * mean_sub / (half_substrate + mean_sub) * mean_oxy / (half_oxygen + mean_oxy)

    own_row = jnp.zeros((1, LANES), jnp.float32)
    for row in range(4):
        own_row = own_row + jnp.where(gz // 8 == row, rate[row : row + 1, :], 0.0)
    rate_row[...] = own_row
    to_scalar = pltpu.make_async_copy(rate_row, rate_smem, local_sem.at[2])
    to_scalar.start()

    arrived(0, bio_recv, DEPTH - 1)
    rows = bio_recv[...].reshape(DEPTH, LANES)
    mine = (lane >> 5) == ((iota(wide, 0) >> 1) & 3)
    for field in range(2):
        turned = rows if field == 0 else pltpu.roll(rows, LANES - 32, 1)
        kept = jnp.where(mine, turned, 0.0)
        for row in range(4):
            mass = jnp.sum(kept[8 * row : 8 * row + 8, :], axis=0, keepdims=True)
            at = field * 4 + row
            d_send[0, at : at + 1, :] = uptake_gain * rate[row : row + 1, :] * mass
    d_send[0, 8:12, :] = rate
    d_send[0, 12:16, :] = jnp.zeros((4, LANES), jnp.float32)
    send(5, col_ids, lambda number: d_send.at[0], d_recv.at[column])
    d_recv[column] = d_send[0]
    send_flows(2)

    to_scalar.wait()

    def rate_of(slot):
        return rate_smem[0, block * 32 + jnp.where(core == 1, 31 - slot, slot)]

    grow_rounds(state_ref, rate_of, mother_ref, turned_ref, growth_ref, daughter_ref, 4)

    arrived(5, d_recv, COLS - 1)
    table_ref[...] = d_recv[...]
    left_here(0, bio_recv, DEPTH - 1)
    left_here(1, a_recv, COLS - 1)
    left_here(2, pair_recv, 1)
    left_here(3, deep_recv, 15)
    left_here(4, pair_recv, 1)
    left_here(5, d_recv, COLS - 1)
    stay.wait()
    for copy in flows:
        copy.wait()


def sweep(sub, oxy, velocity, cell_map, owner, weight, growth, daughter, division, pop, payload):
    f32 = jnp.float32
    shape = jax.ShapeDtypeStruct
    return pl.pallas_call(
        sweep_kernel,
        out_shape=(
            shape((2,) + sub.shape, f32),
            shape(sub.shape, jnp.int32),
            shape((COLS, 16, LANES), f32),
            shape((SUBSTEPS, AGES, SIZES), f32),
            shape((SLOTS + 1, AGES, SIZES), f32),
            shape(payload.shape, f32),
        ),
        in_specs=[VMEM_SPEC] * 9 + [HBM_SPEC] * 2,
        out_specs=(VMEM_SPEC,) * 5 + (HBM_SPEC,),
        scratch_shapes=[
            pltpu.VMEM((2, 8, LANES), f32),
            pltpu.VMEM((2, 8, LANES), f32),
            pltpu.VMEM((2, 2, LANES), f32),
            pltpu.VMEM((2, 2, LANES), f32),
            pltpu.VMEM((2, 2, 32, LANES), f32),
            pltpu.VMEM((64, LANES), jnp.int32),
            pltpu.VMEM((SLOTS + 1, SIZES), f32),
            pltpu.VMEM((SLOTS + 1, SIZES), f32),
            pltpu.VMEM((2, LANES, LANES), f32),
            pltpu.VMEM((COLS, 4, 2 * LANES), f32),
            pltpu.VMEM((COLS, 4, 2 * LANES), f32),
            pltpu.VMEM((2, 4, LANES), f32),
            pltpu.VMEM((2, 4, LANES), f32),
            pltpu.VMEM((1, 4, LANES), f32),
            pltpu.VMEM((16, 4, LANES), f32),
            pltpu.VMEM((1, 1, LANES), f32),
            pltpu.VMEM((DEPTH, 1, LANES), f32),
            pltpu.VMEM((1, 16, LANES), f32),
            pltpu.VMEM((COLS, 16, LANES), f32),
            pltpu.VMEM((1, LANES), f32),
            pltpu.SMEM((1, LANES), f32),
            pltpu.SemaphoreType.DMA((3,)),
            pltpu.SemaphoreType.DMA((8,)),
            pltpu.SemaphoreType.DMA((8,)),
            pltpu.SemaphoreType.DMA((COLS - 1,)),
            pltpu.SemaphoreType.DMA((COLS - 1,)),
            pltpu.SemaphoreType.DMA((6,)),
            pltpu.SemaphoreType.DMA((6,)),
        ],
        compiler_params=pltpu.CompilerParams(
            collective_id=0, has_side_effects=True, vmem_limit_bytes=VMEM_BYTES
        ),
        cost_estimate=pl.CostEstimate(
            flops=3_200_000_000, bytes_accessed=8_000_000, transcendentals=0
        ),
    )(sub, oxy, velocity, cell_map, owner, weight, growth, daughter, division, pop, payload)


def finish_kernel(
    swept_ref,
    pos_ref,
    table_ref,
    list_ref,
    flow_rate_ref,
    growth_ref,
    daughter_ref,
    turned_ref,
    own_ref,
    incoming_ref,
    sub_out_ref,
    oxy_out_ref,
    pop_out_ref,
    state,
    mother_ref,
    rate_rows,
    rate_table,
    rate_list,
    scale_of,
    own_scale,
    target_of,
    state_sem,
    table_sem,
):
    depth = lax.axis_index("gz")
    core = depth & 1
    block = (depth >> 1) & 3
    quarter = depth >> 3

    rows = jnp.zeros((COLS, LANES), jnp.float32)
    for part in range(4):
        rows = rows + jnp.where(quarter == part, table_ref[:, 8 + part, :], 0.0)
    rate_rows[...] = rows
    to_scalar = pltpu.make_async_copy(rate_rows, rate_table, table_sem)
    to_scalar.start()
    to_scalar.wait()

    def scan_own(col, count):
        lowest, highest = list_ref[0, col], list_ref[0, col + 16]

        @pl.when(highest >= 0)
        def _():
            own_scale[lowest >> 4] = flow_rate_ref[lowest & 15]
            own_scale[highest >> 4] = flow_rate_ref[highest & 15]

        return count + jnp.where(highest >= 0, 1, 0) + jnp.where(highest > lowest, 1, 0)

    own = lax.fori_loop(0, COLS, scan_own, jnp.int32(0))

    def scan_arriving(item, count):
        col, rank = item >> 1, item & 1
        lowest, highest = list_ref[0, col + 32], list_ref[0, col + 48]
        key = jnp.where(rank == 0, lowest, highest)
        valid = jnp.where(rank == 0, highest >= 0, highest > lowest)

        @pl.when(valid)
        def _():
            slot = key >> 9
            lane = block * 32 + jnp.where(core == 1, 31 - slot, slot)
            rate_list[count] = rate_table[col, lane]
            scale_of[count] = flow_rate_ref[key & 15]
            target_of[count] = (key >> 4) & 31
            pltpu.make_async_copy(
                incoming_ref.at[col, pl.ds(pl.multiple_of(rank * AGES, AGES), AGES)],
                state.at[count],
                state_sem.at[0],
            ).start()

        return count + jnp.where(valid, 1, 0)

    total = lax.fori_loop(0, 2 * COLS, scan_arriving, jnp.int32(0))

    cells = pos_ref[...].reshape(LANES, LANES)
    low, high = cells & 127, cells >> 7

    def find(col, drawn):
        first, second = drawn
        tile = table_ref[col]
        for part in range(4):
            row = col * 4 + part
            first = lookup(tile[part : part + 1, :], low, high, row, first)
            second = lookup(tile[4 + part : 5 + part, :], low, high, row, second)
        return first, second

    zero = jnp.zeros((LANES, LANES), jnp.float32)
    drawn = lax.fori_loop(0, COLS, find, (zero, zero))
    for field, (out, half) in enumerate(
        ((sub_out_ref, half_substrate), (oxy_out_ref, half_oxygen))
    ):
        swept = swept_ref[field]
        out[...] = swept - drawn[field].reshape(swept.shape) * swept / (half + swept)

    def fetched(slot, carry):
        pltpu.make_async_copy(
            incoming_ref.at[0, pl.ds(0, AGES)], state.at[slot], state_sem.at[0]
        ).wait()
        return carry

    lax.fori_loop(0, total, fetched, 0)
    grow_rounds(
        state,
        lambda slot: rate_list[slot],
        mother_ref,
        turned_ref,
        growth_ref,
        daughter_ref,
        (total + GROUP - 1) // GROUP,
    )

    top = AGES - SUBSTEPS
    for slot in range(SLOTS):

        @pl.when(slot < own)
        def _():
            kept = own_ref[slot]
            kept = kept - own_scale[slot] * kept
            pop_out_ref[slot, :SUBSTEPS, :] = kept[top:]
            pop_out_ref[slot, SUBSTEPS:, :] = kept[:top]

        @pl.when(slot >= own)
        def _():
            pop_out_ref[slot] = jnp.zeros((AGES, SIZES), jnp.float32)

    def arrive(item, carry):
        slot = target_of[item]
        inflow = scale_of[item] * state[item]
        pop_out_ref[slot, :SUBSTEPS, :] = pop_out_ref[slot, :SUBSTEPS, :] + inflow[top:]
        pop_out_ref[slot, SUBSTEPS:, :] = pop_out_ref[slot, SUBSTEPS:, :] + inflow[:top]
        return carry

    lax.fori_loop(0, total, arrive, 0)


def finish(swept, pos, table, lists, flow_rates, growth, daughter, turned, state, incoming):
    f32 = jnp.float32
    field = jax.ShapeDtypeStruct(pos.shape, f32)
    return pl.pallas_call(
        finish_kernel,
        out_shape=(field, field, jax.ShapeDtypeStruct((SLOTS, AGES, SIZES), f32)),
        in_specs=[VMEM_SPEC] * 3 + [SMEM_SPEC] * 2 + [VMEM_SPEC] * 4 + [HBM_SPEC],
        out_specs=(VMEM_SPEC,) * 3,
        scratch_shapes=[
            pltpu.VMEM((SLOTS + 1, AGES, SIZES), f32),
            pltpu.VMEM((SLOTS + 1, SIZES), f32),
            pltpu.VMEM((COLS, LANES), f32),
            pltpu.SMEM((COLS, LANES), f32),
            pltpu.SMEM((32,), f32),
            pltpu.SMEM((32,), f32),
            pltpu.SMEM((32,), f32),
            pltpu.SMEM((32,), jnp.int32),
            pltpu.SemaphoreType.DMA((1,)),
            pltpu.SemaphoreType.DMA,
        ],
        compiler_params=pltpu.CompilerParams(vmem_limit_bytes=VMEM_BYTES),
        cost_estimate=pl.CostEstimate(
            flops=2_000_000_000, bytes_accessed=8_000_000, transcendentals=0
        ),
    )(swept, pos, table, lists, flow_rates, growth, daughter, turned, state, incoming)


def per_device(
    substrate,
    oxygen,
    velocity,
    cell_map,
    owner_slot,
    flow_list,
    flow_rates,
    population,
    growth,
    daughter_kernel,
    division_rate,
    uptake_weight,
):
    owner = owner_slot.reshape(64, LANES)
    lists, payload = prepare(owner, flow_list, population)
    swept, pos, table, turned, state, incoming = sweep(
        substrate,
        oxygen,
        velocity,
        cell_map,
        owner,
        uptake_weight,
        growth,
        daughter_kernel,
        division_rate,
        population,
        payload,
    )
    return finish(
        swept, pos, table, lists, flow_rates, growth, daughter_kernel, turned, state, incoming
    )


def solution(mesh):
    return jax.shard_map(
        per_device,
        mesh=mesh,
        in_specs=(
            P("gz", "gx", "gy"),
            P("gz", "gx", "gy"),
            P(None, "gz", "gx", "gy"),
            P("gz", "gx", "gy"),
            P(),
            P(),
            P(),
            P(("gx", "gy", "gz"), None, None),
            P(),
            P(),
            P(),
            P(),
        ),
        out_specs=(P("gz", "gx", "gy"), P("gz", "gx", "gy"), P(("gx", "gy", "gz"), None, None)),
        check_vma=False,
    )
```

```python
import functools

import jax
import jax.numpy as jnp
from jax import lax
from jax.experimental import pallas as pl
from jax.experimental.pallas import tpu as pltpu
from jax.sharding import PartitionSpec as P

SUBSTEPS = 8
CELLS = 1024
SLOTS = 31
AGES = 64
SIZES = 256
COLS = 16
DEPTH = 32
LANES = 128
GROUP = 8
NONE_KEY = 65536.0

diffusion = 0.05
growth_max = 0.8
half_substrate = 0.3
half_oxygen = 0.1
uptake_gain = 3.0

FLOW_PARTS = (
    ((1, 0), (3, 0), (0, 1), (0, 3)),
    ((2, 0), (0, 2), (1, 1), (3, 3), (1, 3), (3, 1)),
    ((1, 2), (2, 1), (2, 3), (3, 2), (2, 2)),
)

MESH = pl.DeviceIdType.MESH
VMEM_SPEC = pl.BlockSpec(memory_space=pltpu.VMEM)
SMEM_SPEC = pl.BlockSpec(memory_space=pltpu.SMEM)
HBM_SPEC = pl.BlockSpec(memory_space=pltpu.HBM)
VMEM_BYTES = 66_900_000


def iota(shape, dim):
    return lax.broadcasted_iota(jnp.int32, shape, dim)


def device_of(slot):
    return (slot * 33826) >> 20


def lookup(table_row, index, high, row_id, total):
    row = jnp.broadcast_to(table_row, index.shape)
    found = jnp.take_along_axis(row, index, axis=1, mode="promise_in_bounds")
    return jnp.where(high == row_id, found, total)


def grow_rounds(state, rate_of, mother_ref, turned_ref, growth_ref, daughter_ref, groups):
    for step in range(SUBSTEPS):
        oldest = AGES - 1 - step

        def one_group(group, carry, oldest=oldest, step=step):
            base = group * GROUP
            held = state[pl.ds(base, GROUP)]
            moved = jnp.dot(
                held.reshape(GROUP * AGES, SIZES).astype(jnp.bfloat16),
                growth_ref[...],
                preferred_element_type=jnp.float32,
            ).reshape(GROUP, AGES, SIZES)
            for slot in range(GROUP):
                rate = rate_of(base + slot)
                grown = held[slot] + rate * (moved[slot] - held[slot])
                divided = (turned_ref[step] * rate) * grown
                remain = grown - divided
                mother_ref[pl.ds(base + slot, 1), :] = jnp.sum(divided, axis=0, keepdims=True)
                state[base + slot] = remain
                state[base + slot, oldest - 1 : oldest, :] = (
                    remain[oldest - 1 : oldest, :] + remain[oldest : oldest + 1, :]
                )
            return carry

        lax.fori_loop(0, groups, one_group, 0)
        newborn = 2.0 * jnp.dot(
            mother_ref[...].astype(jnp.bfloat16),
            daughter_ref[...],
            preferred_element_type=jnp.float32,
        )
        state[:, oldest, :] = newborn


def list_flows(me, owner_ref, flow_ref, target_ref, index_ref, row_ref):
    for row in range(64):
        lanes = slice(row * LANES, (row + 1) * LANES)
        target_ref[row : row + 1, :] = flow_ref[0:1, lanes]
        index_ref[row : row + 1, :] = flow_ref[1:2, lanes]
    owner = owner_ref[...]
    targets = target_ref[...]
    low, high = targets & 127, targets >> 7
    target_slot = jnp.zeros_like(owner)
    for row in range(64):
        target_slot = lookup(owner_ref[row : row + 1, :], low, high, row, target_slot)
    rate_index = index_ref[...]
    source_dev = device_of(owner)
    source_local = owner - source_dev * SLOTS
    target_dev = device_of(target_slot)
    target_local = target_slot - target_dev * SLOTS
    send_key = (source_local * 16 + rate_index).astype(jnp.float32)
    recv_key = (source_local * 512 + target_local * 16 + rate_index).astype(jnp.float32)
    send_col = jnp.where(source_dev == me, target_dev >> 5, -1)
    recv_col = jnp.where(target_dev == me, source_dev >> 5, -1)
    for col in range(COLS):
        for kind, (key, cols) in enumerate(((send_key, send_col), (recv_key, recv_col))):
            hit = cols == col
            low_row = jnp.min(jnp.where(hit, key, NONE_KEY), axis=0, keepdims=True)
            high_row = jnp.max(jnp.where(hit, key, -1.0), axis=0, keepdims=True)
            at = kind * 32 + col
            row_ref[at : at + 1, :] = low_row
            row_ref[at + 16 : at + 17, :] = high_row
    square = (64, LANES)
    rows = row_ref[...]
    is_low = (iota((64, 1), 0) & 16) == 0
    reduced = jnp.where(
        is_low, jnp.min(rows, axis=1, keepdims=True), jnp.max(rows, axis=1, keepdims=True)
    )
    diagonal = jnp.where(iota(square, 0) == iota(square, 1), reduced, 0.0)
    return jnp.sum(diagonal, axis=0, keepdims=True).astype(jnp.int32)


def sweep_kernel(
    sub_hbm,
    oxy_hbm,
    vel_hbm,
    map_hbm,
    owner_hbm,
    weight_hbm,
    growth_hbm,
    daughter_hbm,
    division_hbm,
    flow_hbm,
    pop_ref,
    fields_ref,
    list_ref,
    rates_ref,
    turned_hbm,
    state_hbm,
    incoming_ref,
    swept_ref,
    pos_ref,
    turned_ref,
    state_ref,
    payload_ref,
    flow_ref,
    target_ref,
    index_ref,
    row_ref,
    list_smem,
    sub_ref,
    oxy_ref,
    vel_ref,
    map_ref,
    owner_ref,
    weight_ref,
    growth_ref,
    daughter_ref,
    division_ref,
    x_send,
    x_recv,
    y_send,
    y_recv,
    z_recv,
    place_ref,
    ages_ref,
    mother_ref,
    value_ref,
    sums_ref,
    a_recv,
    pair_send,
    pair_recv,
    deep_send,
    deep_recv,
    bio_send,
    bio_recv,
    d_send,
    d_recv,
    rate_row,
    rate_smem,
    local_sem,
    halo_send_sem,
    halo_recv_sem,
    flow_send_sem,
    flow_recv_sem,
    send_sem,
    recv_sem,
):
    gx, gy, gz = lax.axis_index("gx"), lax.axis_index("gy"), lax.axis_index("gz")
    column = gx * 4 + gy
    chip, core = gz // 2, lax.rem(gz, 2)
    col_peers = [lax.rem(column + step, COLS) for step in range(1, COLS)]
    col_ids = [(peer // 4, lax.rem(peer, 4), gz) for peer in col_peers]
    deep_ids = [(gx, gy, lax.rem(gz + step, DEPTH)) for step in range(1, DEPTH)]
    same_core_ids = [(gx, gy, lax.rem(gz + step, DEPTH)) for step in range(2, DEPTH, 2)]
    sibling = (gx, gy, gz + 1 - 2 * core)

    pairs = (
        (sub_hbm, sub_ref),
        (oxy_hbm, oxy_ref),
        (map_hbm, map_ref),
        (owner_hbm, owner_ref),
        (weight_hbm, weight_ref),
        (division_hbm, division_ref),
        (vel_hbm, vel_ref),
        (growth_hbm, growth_ref),
        (daughter_hbm, daughter_ref),
        (flow_hbm, flow_ref),
    )
    loads = [
        pltpu.make_async_copy(source, target, local_sem.at[6 + number])
        for number, (source, target) in enumerate(pairs)
    ]
    for copy in loads:
        copy.start()
    barrier = pltpu.get_barrier_semaphore()
    for peer in col_ids + deep_ids:
        pl.semaphore_signal(barrier, inc=1, device_id=peer, device_id_type=MESH)
    load = pltpu.make_async_copy(pop_ref, state_ref.at[pl.ds(0, SLOTS)], local_sem.at[0])
    load.start()

    def send(stage, ids, source_of, target):
        for number, device in enumerate(ids):
            pltpu.make_async_remote_copy(
                src_ref=source_of(number),
                dst_ref=target,
                send_sem=send_sem.at[stage],
                recv_sem=recv_sem.at[stage],
                device_id=device,
                device_id_type=MESH,
            ).start()

    def arrived(stage, buffer, count):
        part = buffer.at[pl.ds(0, count)]
        pltpu.make_async_copy(part, part, recv_sem.at[stage]).wait()

    def left_here(stage, buffer, count):
        part = buffer.at[pl.ds(0, count)]
        pltpu.make_async_copy(part, part, send_sem.at[stage]).wait()

    flows = []

    def send_flows(part):
        for step_x, step_y in FLOW_PARTS[part]:
            near_x, near_y = lax.rem(gx + step_x, 4), lax.rem(gy + step_y, 4)
            number = len(flows)
            copy = pltpu.make_async_remote_copy(
                src_ref=payload_ref.at[near_x * 4 + near_y],
                dst_ref=incoming_ref.at[column],
                send_sem=flow_send_sem.at[number],
                recv_sem=flow_recv_sem.at[number],
                device_id=(near_x, near_y, gz),
                device_id_type=MESH,
            )
            copy.start()
            flows.append(copy)

    for copy in loads[:2]:
        copy.wait()
    fields = (sub_ref, oxy_ref)
    for field, ref in enumerate(fields):
        layers = slice(field * 4, field * 4 + 4)
        x_send[0, layers, :] = ref[:, 0, :]
        x_send[1, layers, :] = ref[:, 31, :]
        turned = ref[...].reshape(LANES, LANES).T
        y_send[0, field : field + 1, :] = turned[0:1, :]
        y_send[1, field : field + 1, :] = turned[LANES - 1 : LANES, :]

    for copy in loads[2:]:
        copy.wait()
    list_ref[...] = list_flows(
        column * DEPTH + gz, owner_ref, flow_ref, target_ref, index_ref, row_ref
    )
    list_copy = pltpu.make_async_copy(list_ref, list_smem, local_sem.at[1])
    list_copy.start()
    owner = owner_ref[...]
    owner_dev = device_of(owner)
    owner_local = owner - owner_dev * SLOTS
    place_ref[...] = (owner_dev >> 1) * 32 + jnp.where(
        (owner_dev & 1) == 1, 31 - owner_local, owner_local
    )
    pl.semaphore_wait(barrier, len(col_ids) + len(deep_ids))

    halos = []
    for side in range(2):
        step = 3 if side == 0 else 1
        near_x = (lax.rem(gx + step, 4), gy, gz)
        near_y = (gx, lax.rem(gy + step, 4), gz)
        near_z = (gx, gy, lax.rem(gz + (DEPTH - 1 if side == 0 else 1), DEPTH))
        layer = 0 if side == 0 else 3
        pairs = [
            (x_send.at[side], x_recv.at[1 - side], near_x),
            (y_send.at[side], y_recv.at[1 - side], near_y),
            (sub_ref.at[layer], z_recv.at[1 - side, 0], near_z),
            (oxy_ref.at[layer], z_recv.at[1 - side, 1], near_z),
        ]
        for number, (source, target, device) in enumerate(pairs):
            sem = side * 4 + number
            halos.append(
                pltpu.make_async_remote_copy(
                    src_ref=source,
                    dst_ref=target,
                    send_sem=halo_send_sem.at[sem],
                    recv_sem=halo_recv_sem.at[sem],
                    device_id=device,
                    device_id_type=MESH,
                )
            )
    for copy in halos:
        copy.start()

    load.wait()
    state_ref[SLOTS] = jnp.zeros((AGES, SIZES), jnp.float32)
    for slot in range(SLOTS + 1):
        ages_ref[slot : slot + 1, :] = jnp.sum(state_ref[slot], axis=0, keepdims=True)
    summed = ages_ref[...]
    owned = jnp.where(owner_dev == column * DEPTH + gz, 1.0, 0.0)
    held = jnp.sum(jnp.sum(owned, axis=0, keepdims=True), axis=1, keepdims=True)
    block = lax.rem(chip, 4)
    wide = (DEPTH, LANES)
    lane = iota(wide, 1)
    local = lane & 31
    slot_of_lane = jnp.where(core == 1, 31 - local, local)
    here = ((lane >> 5) == block) & (slot_of_lane == iota(wide, 0))
    here = here & (slot_of_lane.astype(jnp.float32) < held)
    masses = []
    for field in range(2):
        weighted = summed * weight_ref[field : field + 1, :]
        mass = jnp.sum(weighted, axis=1, keepdims=True) / (AGES * SIZES)
        masses.append(jnp.sum(jnp.where(here, mass, 0.0), axis=0, keepdims=True))
    packed = masses[0] + pltpu.roll(masses[1], 32, 1)
    bio_send[0] = packed
    bio_recv[gz] = packed
    send(0, deep_ids, lambda number: bio_send.at[0], bio_recv.at[gz])

    list_copy.wait()

    def pack(col, carry):
        lowest, highest = list_smem[0, col], list_smem[0, col + 16]
        first = jnp.where(highest >= 0, (lowest >> 4) & 31, 0)
        second = jnp.where(highest >= 0, (highest >> 4) & 31, 0)
        payload_ref[col, :AGES, :] = state_ref[first]
        payload_ref[col, AGES:, :] = state_ref[second]
        return carry

    lax.fori_loop(0, COLS, pack, 0)
    stay = pltpu.make_async_copy(
        payload_ref.at[column], incoming_ref.at[column], local_sem.at[2]
    )
    stay.start()

    cells = map_ref[...].reshape(LANES, LANES)
    low, high = cells & 127, cells >> 7

    def find(step, total):
        for part in range(8):
            row = step * 8 + part
            total = lookup(place_ref[pl.ds(row, 1), :], low, high, row, total)
        return total

    place = lax.fori_loop(0, 8, find, jnp.zeros_like(cells))
    pos_ref[...] = place.reshape(pos_ref.shape)

    division = division_ref[...]
    turned_ref[0] = division
    for step in range(1, SUBSTEPS):
        turned_ref[step] = pltpu.roll(division, AGES - step, 0)
    turned_out = pltpu.make_async_copy(turned_ref, turned_hbm, local_sem.at[3])
    turned_out.start()

    for copy in halos:
        copy.wait()
    send_flows(0)

    shape = (4, 32, LANES)
    row_id = iota(shape, 1)
    lane_id = iota(shape, 2)
    inside = [
        (jnp.where(at > 0, 1.0, 0.0), jnp.where(at < count - 1, 1.0, 0.0))
        for at, count in ((gz, DEPTH), (gx, 4), (gy, 4))
    ]
    for field, ref in enumerate(fields):
        center = ref[...]
        layers = slice(field * 4, field * 4 + 4)
        z_low = (z_recv[0, field] * inside[0][0])[None]
        z_high = (z_recv[1, field] * inside[0][1])[None]
        x_low = (x_recv[0, layers, :] * inside[1][0])[:, None, :]
        x_high = (x_recv[1, layers, :] * inside[1][1])[:, None, :]
        y_edges = []
        for side in range(2):
            edge = y_recv[side, field : field + 1, :] * inside[2][side]
            y_edges.append(jnp.broadcast_to(edge, (LANES, LANES)).T.reshape(shape))
        lower = (
            jnp.concatenate([z_low, center[:3]], axis=0),
            jnp.where(row_id == 0, x_low, pltpu.roll(center, 1, 1)),
            jnp.where(lane_id == 0, y_edges[0], pltpu.roll(center, 1, 2)),
        )
        upper = (
            jnp.concatenate([center[1:], z_high], axis=0),
            jnp.where(row_id == 31, x_high, pltpu.roll(center, 31, 1)),
            jnp.where(lane_id == LANES - 1, y_edges[1], pltpu.roll(center, LANES - 1, 2)),
        )
        total = center
        for axis in range(3):
            courant = vel_ref[axis]
            total = total + diffusion * (lower[axis] + upper[axis] - 2.0 * center)
            total = total - jnp.maximum(courant, 0.0) * (center - lower[axis])
            total = total - jnp.minimum(courant, 0.0) * (upper[axis] - center)
        swept_ref[field] = total
        value_ref[field] = total.reshape(LANES, LANES)

    fine_row = iota((2 * LANES, LANES), 0)
    sub_row = iota((64, LANES), 0)
    row_half = sub_row >> 1
    even = (sub_row & 1) == 0

    def gather_sums(step, total):
        rows = pl.ds(pl.multiple_of(step * 8, 8), 8)
        place = pos_ref[step // 4, pl.ds(pl.multiple_of(lax.rem(step, 4) * 8, 8), 8), :]
        first = value_ref[0, rows, :]
        second = value_ref[1, rows, :]
        left, right = [], []
        for row in range(8):
            one = slice(row, row + 1)
            value = jnp.where(even, first[one], second[one])
            coarse = value.astype(jnp.bfloat16).astype(jnp.float32)
            hit = (place[one] >> 8) == row_half
            top = jnp.where(hit, coarse, 0.0).astype(jnp.bfloat16)
            rest = jnp.where(hit, value - coarse, 0.0).astype(jnp.bfloat16)
            left.append(jnp.concatenate([top, rest], axis=0))
            right.append(jnp.where((place[one] & 255) == fine_row, 1.0, 0.0).astype(jnp.bfloat16))
        return total + lax.dot_general(
            jnp.concatenate(left, axis=1),
            jnp.concatenate(right, axis=1),
            (((1,), (1,)), ((), ())),
            preferred_element_type=jnp.float32,
        )

    sums = lax.fori_loop(0, 16, gather_sums, jnp.zeros((LANES, 2 * LANES), jnp.float32))
    sums_ref[...] = (sums[:64] + sums[64:]).reshape(COLS, 4, 2 * LANES)

    send(1, col_ids, lambda number: sums_ref.at[col_peers[number]], a_recv.at[column])
    a_recv[column] = sums_ref[column]
    arrived(1, a_recv, COLS - 1)
    send_flows(1)
    part = jnp.sum(a_recv[...], axis=0)
    split = []
    for field in range(2):
        split.append(
            jnp.concatenate(
                [
                    part[2 * (row // 2) + field : 2 * (row // 2) + field + 1][
                        :, (row % 2) * LANES : (row % 2 + 1) * LANES
                    ]
                    for row in range(4)
                ],
                axis=0,
            )
        )

    first_core = core == 0
    pair_send[0] = jnp.where(first_core, split[1], split[0])
    send(2, [sibling], lambda number: pair_send.at[0], pair_recv.at[0])
    arrived(2, pair_recv, 1)
    chip_sum = jnp.where(first_core, split[0], split[1]) + pair_recv[0]
    deep_send[0] = chip_sum
    send(3, same_core_ids, lambda number: deep_send.at[0], deep_recv.at[chip])
    deep_recv[chip] = chip_sum
    arrived(3, deep_recv, 15)
    added = jnp.sum(deep_recv[...], axis=0)
    pair_send[1] = added
    send(4, [sibling], lambda number: pair_send.at[1], pair_recv.at[1])
    arrived(4, pair_recv, 1)
    other = pair_recv[1]
    mean_sub = jnp.where(first_core, added, other) / CELLS
    mean_oxy = jnp.where(first_core, other, added) / CELLS
    rate = growth_max * mean_sub / (half_substrate + mean_sub) * mean_oxy / (half_oxygen + mean_oxy)

    own_row = jnp.zeros((1, LANES), jnp.float32)
    for row in range(4):
        own_row = own_row + jnp.where(gz // 8 == row, rate[row : row + 1, :], 0.0)
    rate_row[...] = own_row
    to_scalar = pltpu.make_async_copy(rate_row, rate_smem, local_sem.at[4])
    to_scalar.start()

    arrived(0, bio_recv, DEPTH - 1)
    rows = bio_recv[...].reshape(DEPTH, LANES)
    mine = (lane >> 5) == ((iota(wide, 0) >> 1) & 3)
    for field in range(2):
        turned = rows if field == 0 else pltpu.roll(rows, LANES - 32, 1)
        kept = jnp.where(mine, turned, 0.0)
        for row in range(4):
            mass = jnp.sum(kept[8 * row : 8 * row + 8, :], axis=0, keepdims=True)
            at = field * 4 + row
            d_send[0, at : at + 1, :] = uptake_gain * rate[row : row + 1, :] * mass
    d_send[0, 8:12, :] = rate
    d_send[0, 12:16, :] = jnp.zeros((4, LANES), jnp.float32)
    send(5, col_ids, lambda number: d_send.at[0], d_recv.at[column])
    d_recv[column] = d_send[0]
    send_flows(2)

    to_scalar.wait()

    def rate_of(slot):
        return rate_smem[0, block * 32 + jnp.where(core == 1, 31 - slot, slot)]

    grow_rounds(state_ref, rate_of, mother_ref, turned_ref, growth_ref, daughter_ref, 4)

    state_out = pltpu.make_async_copy(state_ref, state_hbm, local_sem.at[5])
    state_out.start()

    arrived(5, d_recv, COLS - 1)
    rates = jnp.zeros((COLS, LANES), jnp.float32)
    for row in range(4):
        rates = rates + jnp.where(gz // 8 == row, d_recv[:, 8 + row, :], 0.0)
    rates_ref[...] = rates

    cells = pos_ref[...].reshape(LANES, LANES)
    low, high = cells & 127, cells >> 7

    def draw(col, drawn):
        first, second = drawn
        tile = d_recv[col]
        for part in range(4):
            row = col * 4 + part
            first = lookup(tile[part : part + 1, :], low, high, row, first)
            second = lookup(tile[4 + part : 5 + part, :], low, high, row, second)
        return first, second

    zero = jnp.zeros((LANES, LANES), jnp.float32)
    drawn = lax.fori_loop(0, COLS, draw, (zero, zero))
    for field, half in enumerate((half_substrate, half_oxygen)):
        swept = swept_ref[field]
        fields_ref[field] = swept - drawn[field].reshape(shape) * swept / (half + swept)

    turned_out.wait()
    state_out.wait()
    left_here(0, bio_recv, DEPTH - 1)
    left_here(1, a_recv, COLS - 1)
    left_here(2, pair_recv, 1)
    left_here(3, deep_recv, 15)
    left_here(4, pair_recv, 1)
    left_here(5, d_recv, COLS - 1)
    stay.wait()
    for copy in flows:
        copy.wait()


def sweep(sub, oxy, velocity, cell_map, owner, weight, growth, daughter, division, flow, pop):
    f32 = jnp.float32
    shape = jax.ShapeDtypeStruct
    return pl.pallas_call(
        sweep_kernel,
        out_shape=(
            shape((2,) + sub.shape, f32),
            shape((1, LANES), jnp.int32),
            shape((COLS, LANES), f32),
            shape((SUBSTEPS, AGES, SIZES), f32),
            shape((SLOTS + 1, AGES, SIZES), f32),
            shape((COLS, 2 * AGES, SIZES), f32),
        ),
        in_specs=[HBM_SPEC] * 11,
        out_specs=(VMEM_SPEC,) * 3 + (HBM_SPEC,) * 3,
        scratch_shapes=[
            pltpu.VMEM((2,) + sub.shape, f32),
            pltpu.VMEM(sub.shape, jnp.int32),
            pltpu.VMEM((SUBSTEPS, AGES, SIZES), f32),
            pltpu.VMEM((SLOTS + 1, AGES, SIZES), f32),
            pltpu.VMEM((COLS, 2 * AGES, SIZES), f32),
            pltpu.VMEM(flow.shape, jnp.int32),
            pltpu.VMEM((64, LANES), jnp.int32),
            pltpu.VMEM((64, LANES), jnp.int32),
            pltpu.VMEM((64, LANES), f32),
            pltpu.SMEM((1, LANES), jnp.int32),
            pltpu.VMEM(sub.shape, f32),
            pltpu.VMEM(sub.shape, f32),
            pltpu.VMEM(velocity.shape, f32),
            pltpu.VMEM(sub.shape, jnp.int32),
            pltpu.VMEM((64, LANES), jnp.int32),
            pltpu.VMEM(weight.shape, f32),
            pltpu.VMEM(growth.shape, growth.dtype),
            pltpu.VMEM(daughter.shape, daughter.dtype),
            pltpu.VMEM(division.shape, f32),
            pltpu.VMEM((2, 8, LANES), f32),
            pltpu.VMEM((2, 8, LANES), f32),
            pltpu.VMEM((2, 2, LANES), f32),
            pltpu.VMEM((2, 2, LANES), f32),
            pltpu.VMEM((2, 2, 32, LANES), f32),
            pltpu.VMEM((64, LANES), jnp.int32),
            pltpu.VMEM((SLOTS + 1, SIZES), f32),
            pltpu.VMEM((SLOTS + 1, SIZES), f32),
            pltpu.VMEM((2, LANES, LANES), f32),
            pltpu.VMEM((COLS, 4, 2 * LANES), f32),
            pltpu.VMEM((COLS, 4, 2 * LANES), f32),
            pltpu.VMEM((2, 4, LANES), f32),
            pltpu.VMEM((2, 4, LANES), f32),
            pltpu.VMEM((1, 4, LANES), f32),
            pltpu.VMEM((16, 4, LANES), f32),
            pltpu.VMEM((1, 1, LANES), f32),
            pltpu.VMEM((DEPTH, 1, LANES), f32),
            pltpu.VMEM((1, 16, LANES), f32),
            pltpu.VMEM((COLS, 16, LANES), f32),
            pltpu.VMEM((1, LANES), f32),
            pltpu.SMEM((1, LANES), f32),
            pltpu.SemaphoreType.DMA((16,)),
            pltpu.SemaphoreType.DMA((8,)),
            pltpu.SemaphoreType.DMA((8,)),
            pltpu.SemaphoreType.DMA((COLS - 1,)),
            pltpu.SemaphoreType.DMA((COLS - 1,)),
            pltpu.SemaphoreType.DMA((6,)),
            pltpu.SemaphoreType.DMA((6,)),
        ],
        compiler_params=pltpu.CompilerParams(
            collective_id=0, has_side_effects=True, vmem_limit_bytes=VMEM_BYTES
        ),
        cost_estimate=pl.CostEstimate(
            flops=3_200_000_000, bytes_accessed=8_000_000, transcendentals=0
        ),
    )(sub, oxy, velocity, cell_map, owner, weight, growth, daughter, division, flow, pop)


def finish_kernel(
    list_ref,
    rate_table,
    flow_rate_ref,
    fields_hbm,
    own_hbm,
    growth_hbm,
    daughter_hbm,
    turned_hbm,
    incoming_ref,
    sub_out_ref,
    oxy_out_ref,
    pop_out_ref,
    own_ref,
    growth_ref,
    daughter_ref,
    turned_ref,
    state,
    mother_ref,
    rate_list,
    scale_of,
    own_scale,
    target_of,
    load_sem,
    state_sem,
):
    depth = lax.axis_index("gz")
    core = depth & 1
    block = (depth >> 1) & 3
    pairs = (
        (own_hbm, own_ref),
        (growth_hbm, growth_ref),
        (daughter_hbm, daughter_ref),
        (turned_hbm, turned_ref),
        (fields_hbm.at[0], sub_out_ref),
        (fields_hbm.at[1], oxy_out_ref),
    )
    loads = [
        pltpu.make_async_copy(source, target, load_sem.at[number])
        for number, (source, target) in enumerate(pairs)
    ]
    for copy in loads:
        copy.start()

    def scan_arriving(item, count):
        col, rank = item >> 1, item & 1
        lowest, highest = list_ref[0, col + 32], list_ref[0, col + 48]
        key = jnp.where(rank == 0, lowest, highest)
        valid = jnp.where(rank == 0, highest >= 0, highest > lowest)

        @pl.when(valid)
        def _():
            slot = key >> 9
            lane = block * 32 + jnp.where(core == 1, 31 - slot, slot)
            rate_list[count] = rate_table[col, lane]
            scale_of[count] = flow_rate_ref[key & 15]
            target_of[count] = (key >> 4) & 31
            pltpu.make_async_copy(
                incoming_ref.at[col, pl.ds(pl.multiple_of(rank * AGES, AGES), AGES)],
                state.at[count],
                state_sem.at[0],
            ).start()

        return count + jnp.where(valid, 1, 0)

    total = lax.fori_loop(0, 2 * COLS, scan_arriving, jnp.int32(0))

    def scan_own(col, count):
        lowest, highest = list_ref[0, col], list_ref[0, col + 16]

        @pl.when(highest >= 0)
        def _():
            own_scale[lowest >> 4] = flow_rate_ref[lowest & 15]
            own_scale[highest >> 4] = flow_rate_ref[highest & 15]

        return count + jnp.where(highest >= 0, 1, 0) + jnp.where(highest > lowest, 1, 0)

    own = lax.fori_loop(0, COLS, scan_own, jnp.int32(0))
    for copy in loads:
        copy.wait()

    top = AGES - SUBSTEPS
    for slot in range(SLOTS):

        @pl.when(slot < own)
        def _():
            kept = own_ref[slot]
            kept = kept - own_scale[slot] * kept
            pop_out_ref[slot, :SUBSTEPS, :] = kept[top:]
            pop_out_ref[slot, SUBSTEPS:, :] = kept[:top]

        @pl.when(slot >= own)
        def _():
            pop_out_ref[slot] = jnp.zeros((AGES, SIZES), jnp.float32)

    def fetched(slot, carry):
        pltpu.make_async_copy(
            incoming_ref.at[0, pl.ds(0, AGES)], state.at[slot], state_sem.at[0]
        ).wait()
        return carry

    lax.fori_loop(0, total, fetched, 0)
    grow_rounds(
        state,
        lambda slot: rate_list[slot],
        mother_ref,
        turned_ref,
        growth_ref,
        daughter_ref,
        (total + GROUP - 1) // GROUP,
    )

    def arrive(item, carry):
        slot = target_of[item]
        inflow = scale_of[item] * state[item]
        pop_out_ref[slot, :SUBSTEPS, :] = pop_out_ref[slot, :SUBSTEPS, :] + inflow[top:]
        pop_out_ref[slot, SUBSTEPS:, :] = pop_out_ref[slot, SUBSTEPS:, :] + inflow[:top]
        return carry

    lax.fori_loop(0, total, arrive, 0)


def finish(lists, rates, flow_rates, fields, state, growth, daughter, turned, incoming):
    f32 = jnp.float32
    field = jax.ShapeDtypeStruct(fields.shape[1:], f32)
    return pl.pallas_call(
        finish_kernel,
        out_shape=(field, field, jax.ShapeDtypeStruct((SLOTS, AGES, SIZES), f32)),
        in_specs=[SMEM_SPEC] * 3 + [HBM_SPEC] * 6,
        out_specs=(VMEM_SPEC,) * 3,
        scratch_shapes=[
            pltpu.VMEM(state.shape, f32),
            pltpu.VMEM(growth.shape, growth.dtype),
            pltpu.VMEM(daughter.shape, daughter.dtype),
            pltpu.VMEM(turned.shape, f32),
            pltpu.VMEM((SLOTS + 1, AGES, SIZES), f32),
            pltpu.VMEM((SLOTS + 1, SIZES), f32),
            pltpu.SMEM((32,), f32),
            pltpu.SMEM((32,), f32),
            pltpu.SMEM((32,), f32),
            pltpu.SMEM((32,), jnp.int32),
            pltpu.SemaphoreType.DMA((6,)),
            pltpu.SemaphoreType.DMA((1,)),
        ],
        compiler_params=pltpu.CompilerParams(vmem_limit_bytes=VMEM_BYTES),
        cost_estimate=pl.CostEstimate(
            flops=2_000_000_000, bytes_accessed=8_000_000, transcendentals=0
        ),
    )(lists, rates, flow_rates, fields, state, growth, daughter, turned, incoming)


def per_device(
    substrate,
    oxygen,
    velocity,
    cell_map,
    owner_slot,
    flow_list,
    flow_rates,
    population,
    growth,
    daughter_kernel,
    division_rate,
    uptake_weight,
):
    fields, lists, rates, turned, state, incoming = sweep(
        substrate,
        oxygen,
        velocity,
        cell_map,
        owner_slot.reshape(64, LANES),
        uptake_weight,
        growth,
        daughter_kernel,
        division_rate,
        flow_list,
        population,
    )
    return finish(
        lists, rates, flow_rates, fields, state, growth, daughter_kernel, turned, incoming
    )


def solution(mesh):
    return jax.shard_map(
        per_device,
        mesh=mesh,
        in_specs=(
            P("gz", "gx", "gy"),
            P("gz", "gx", "gy"),
            P(None, "gz", "gx", "gy"),
            P("gz", "gx", "gy"),
            P(),
            P(),
            P(),
            P(("gx", "gy", "gz"), None, None),
            P(),
            P(),
            P(),
            P(),
        ),
        out_specs=(P("gz", "gx", "gy"), P("gz", "gx", "gy"), P(("gx", "gy", "gz"), None, None)),
        check_vma=False,
    )
```

```python
import functools

import jax
import jax.numpy as jnp
from jax import lax
from jax.experimental import pallas as pl
from jax.experimental.pallas import tpu as pltpu
from jax.sharding import PartitionSpec as P

SUBSTEPS = 8
CELLS = 1024
SLOTS = 31
AGES = 64
SIZES = 256
COLS = 16
DEPTH = 32
LANES = 128
GROUP = 8
NONE_KEY = 65536.0

diffusion = 0.05
growth_max = 0.8
half_substrate = 0.3
half_oxygen = 0.1
uptake_gain = 3.0

FLOW_PARTS = (
    ((1, 0), (3, 0), (0, 1), (0, 3), (2, 0), (0, 2)),
    ((1, 1), (3, 3), (1, 3), (3, 1), (1, 2)),
    ((2, 1), (2, 3), (3, 2), (2, 2)),
)

MESH = pl.DeviceIdType.MESH
VMEM_SPEC = pl.BlockSpec(memory_space=pltpu.VMEM)
SMEM_SPEC = pl.BlockSpec(memory_space=pltpu.SMEM)
HBM_SPEC = pl.BlockSpec(memory_space=pltpu.HBM)
VMEM_BYTES = 66_900_000


def iota(shape, dim):
    return lax.broadcasted_iota(jnp.int32, shape, dim)


def device_of(slot):
    return (slot * 33826) >> 20


def lookup(table_row, index, high, row_id, total):
    row = jnp.broadcast_to(table_row, index.shape)
    found = jnp.take_along_axis(row, index, axis=1, mode="promise_in_bounds")
    return jnp.where(high == row_id, found, total)


def grow_rounds(state, rate_of, mother_ref, turned_ref, growth_ref, daughter_ref, groups):
    for step in range(SUBSTEPS):
        oldest = AGES - 1 - step

        def one_group(group, carry, oldest=oldest, step=step):
            base = group * GROUP
            held = state[pl.ds(base, GROUP)]
            moved = jnp.dot(
                held.reshape(GROUP * AGES, SIZES).astype(jnp.bfloat16),
                growth_ref[...],
                preferred_element_type=jnp.float32,
            ).reshape(GROUP, AGES, SIZES)
            for slot in range(GROUP):
                rate = rate_of(base + slot)
                grown = held[slot] + rate * (moved[slot] - held[slot])
                divided = (turned_ref[step] * rate) * grown
                remain = grown - divided
                mother_ref[pl.ds(base + slot, 1), :] = jnp.sum(divided, axis=0, keepdims=True)
                state[base + slot] = remain
                state[base + slot, oldest - 1 : oldest, :] = (
                    remain[oldest - 1 : oldest, :] + remain[oldest : oldest + 1, :]
                )
            return carry

        lax.fori_loop(0, groups, one_group, 0)
        newborn = 2.0 * jnp.dot(
            mother_ref[...].astype(jnp.bfloat16),
            daughter_ref[...],
            preferred_element_type=jnp.float32,
        )
        state[:, oldest, :] = newborn


def list_flows(me, owner_ref, flow_ref, target_ref, index_ref, row_ref):
    for row in range(64):
        lanes = slice(row * LANES, (row + 1) * LANES)
        target_ref[row : row + 1, :] = flow_ref[0:1, lanes]
        index_ref[row : row + 1, :] = flow_ref[1:2, lanes]
    owner = owner_ref[...]
    targets = target_ref[...]
    low, high = targets & 127, targets >> 7
    target_slot = jnp.zeros_like(owner)
    for row in range(64):
        target_slot = lookup(owner_ref[row : row + 1, :], low, high, row, target_slot)
    rate_index = index_ref[...]
    source_dev = device_of(owner)
    source_local = owner - source_dev * SLOTS
    target_dev = device_of(target_slot)
    target_local = target_slot - target_dev * SLOTS
    send_key = (source_local * 16 + rate_index).astype(jnp.float32)
    recv_key = (source_local * 512 + target_local * 16 + rate_index).astype(jnp.float32)
    send_col = jnp.where(source_dev == me, target_dev >> 5, -1)
    recv_col = jnp.where(target_dev == me, source_dev >> 5, -1)
    for col in range(COLS):
        for kind, (key, cols) in enumerate(((send_key, send_col), (recv_key, recv_col))):
            hit = cols == col
            low_row = jnp.min(jnp.where(hit, key, NONE_KEY), axis=0, keepdims=True)
            high_row = jnp.max(jnp.where(hit, key, -1.0), axis=0, keepdims=True)
            at = kind * 32 + col
            row_ref[at : at + 1, :] = low_row
            row_ref[at + 16 : at + 17, :] = high_row
    square = (64, LANES)
    rows = row_ref[...]
    is_low = (iota((64, 1), 0) & 16) == 0
    reduced = jnp.where(
        is_low, jnp.min(rows, axis=1, keepdims=True), jnp.max(rows, axis=1, keepdims=True)
    )
    diagonal = jnp.where(iota(square, 0) == iota(square, 1), reduced, 0.0)
    return jnp.sum(diagonal, axis=0, keepdims=True).astype(jnp.int32)


def sweep_kernel(
    sub_hbm,
    oxy_hbm,
    vel_hbm,
    map_hbm,
    owner_hbm,
    weight_hbm,
    growth_hbm,
    daughter_hbm,
    division_hbm,
    flow_hbm,
    pop_ref,
    fields_ref,
    list_ref,
    rates_ref,
    turned_hbm,
    state_hbm,
    incoming_ref,
    swept_ref,
    pos_ref,
    turned_ref,
    state_ref,
    payload_ref,
    flow_ref,
    target_ref,
    index_ref,
    row_ref,
    list_smem,
    sub_ref,
    oxy_ref,
    vel_ref,
    map_ref,
    owner_ref,
    weight_ref,
    growth_ref,
    daughter_ref,
    division_ref,
    x_send,
    x_recv,
    y_send,
    y_recv,
    z_recv,
    place_ref,
    ages_ref,
    mother_ref,
    value_ref,
    sums_ref,
    a_recv,
    pair_send,
    pair_recv,
    deep_send,
    deep_recv,
    bio_send,
    bio_recv,
    d_send,
    d_recv,
    rate_row,
    rate_smem,
    local_sem,
    halo_send_sem,
    halo_recv_sem,
    flow_send_sem,
    flow_recv_sem,
    send_sem,
    recv_sem,
):
    gx, gy, gz = lax.axis_index("gx"), lax.axis_index("gy"), lax.axis_index("gz")
    column = gx * 4 + gy
    chip, core = gz // 2, lax.rem(gz, 2)
    col_peers = [lax.rem(column + step, COLS) for step in range(1, COLS)]
    col_ids = [(peer // 4, lax.rem(peer, 4), gz) for peer in col_peers]
    deep_ids = [(gx, gy, lax.rem(gz + step, DEPTH)) for step in range(1, DEPTH)]
    same_core_ids = [(gx, gy, lax.rem(gz + step, DEPTH)) for step in range(2, DEPTH, 2)]
    sibling = (gx, gy, gz + 1 - 2 * core)

    pairs = (
        (sub_hbm, sub_ref),
        (oxy_hbm, oxy_ref),
        (map_hbm, map_ref),
        (owner_hbm, owner_ref),
        (weight_hbm, weight_ref),
        (division_hbm, division_ref),
        (vel_hbm, vel_ref),
        (growth_hbm, growth_ref),
        (daughter_hbm, daughter_ref),
        (flow_hbm, flow_ref),
    )
    loads = [
        pltpu.make_async_copy(source, target, local_sem.at[6 + number])
        for number, (source, target) in enumerate(pairs)
    ]
    for copy in loads:
        copy.start()
    barrier = pltpu.get_barrier_semaphore()
    for peer in col_ids + deep_ids:
        pl.semaphore_signal(barrier, inc=1, device_id=peer, device_id_type=MESH)
    load = pltpu.make_async_copy(pop_ref, state_ref.at[pl.ds(0, SLOTS)], local_sem.at[0])
    load.start()

    def send(stage, ids, source_of, target):
        for number, device in enumerate(ids):
            pltpu.make_async_remote_copy(
                src_ref=source_of(number),
                dst_ref=target,
                send_sem=send_sem.at[stage],
                recv_sem=recv_sem.at[stage],
                device_id=device,
                device_id_type=MESH,
            ).start()

    def arrived(stage, buffer, count):
        part = buffer.at[pl.ds(0, count)]
        pltpu.make_async_copy(part, part, recv_sem.at[stage]).wait()

    def left_here(stage, buffer, count):
        part = buffer.at[pl.ds(0, count)]
        pltpu.make_async_copy(part, part, send_sem.at[stage]).wait()

    flows = []

    def send_flows(part):
        for step_x, step_y in FLOW_PARTS[part]:
            near_x, near_y = lax.rem(gx + step_x, 4), lax.rem(gy + step_y, 4)
            number = len(flows)
            copy = pltpu.make_async_remote_copy(
                src_ref=payload_ref.at[near_x * 4 + near_y],
                dst_ref=incoming_ref.at[column],
                send_sem=flow_send_sem.at[number],
                recv_sem=flow_recv_sem.at[number],
                device_id=(near_x, near_y, gz),
                device_id_type=MESH,
            )
            copy.start()
            flows.append(copy)

    for copy in loads[:2]:
        copy.wait()
    fields = (sub_ref, oxy_ref)
    for field, ref in enumerate(fields):
        layers = slice(field * 4, field * 4 + 4)
        x_send[0, layers, :] = ref[:, 0, :]
        x_send[1, layers, :] = ref[:, 31, :]
        turned = ref[...].reshape(LANES, LANES).T
        y_send[0, field : field + 1, :] = turned[0:1, :]
        y_send[1, field : field + 1, :] = turned[LANES - 1 : LANES, :]

    for copy in loads[2:]:
        copy.wait()
    list_ref[...] = list_flows(
        column * DEPTH + gz, owner_ref, flow_ref, target_ref, index_ref, row_ref
    )
    list_copy = pltpu.make_async_copy(list_ref, list_smem, local_sem.at[1])
    list_copy.start()
    owner = owner_ref[...]
    owner_dev = device_of(owner)
    owner_local = owner - owner_dev * SLOTS
    place_ref[...] = (owner_dev >> 1) * 32 + jnp.where(
        (owner_dev & 1) == 1, 31 - owner_local, owner_local
    )
    pl.semaphore_wait(barrier, len(col_ids) + len(deep_ids))

    halos = []
    for side in range(2):
        step = 3 if side == 0 else 1
        near_x = (lax.rem(gx + step, 4), gy, gz)
        near_y = (gx, lax.rem(gy + step, 4), gz)
        near_z = (gx, gy, lax.rem(gz + (DEPTH - 1 if side == 0 else 1), DEPTH))
        layer = 0 if side == 0 else 3
        pairs = [
            (x_send.at[side], x_recv.at[1 - side], near_x),
            (y_send.at[side], y_recv.at[1 - side], near_y),
            (sub_ref.at[layer], z_recv.at[1 - side, 0], near_z),
            (oxy_ref.at[layer], z_recv.at[1 - side, 1], near_z),
        ]
        for number, (source, target, device) in enumerate(pairs):
            sem = side * 4 + number
            halos.append(
                pltpu.make_async_remote_copy(
                    src_ref=source,
                    dst_ref=target,
                    send_sem=halo_send_sem.at[sem],
                    recv_sem=halo_recv_sem.at[sem],
                    device_id=device,
                    device_id_type=MESH,
                )
            )
    for copy in halos:
        copy.start()

    load.wait()
    list_copy.wait()

    def pack(col, carry):
        lowest, highest = list_smem[0, col], list_smem[0, col + 16]
        first = jnp.where(highest >= 0, (lowest >> 4) & 31, 0)
        second = jnp.where(highest >= 0, (highest >> 4) & 31, 0)
        payload_ref[col, :AGES, :] = state_ref[first]
        payload_ref[col, AGES:, :] = state_ref[second]
        return carry

    lax.fori_loop(0, COLS, pack, 0)
    stay = pltpu.make_async_copy(
        payload_ref.at[column], incoming_ref.at[column], local_sem.at[2]
    )
    stay.start()
    send_flows(0)

    cells = map_ref[...].reshape(LANES, LANES)
    low, high = cells & 127, cells >> 7

    def find(step, total):
        for part in range(8):
            row = step * 8 + part
            total = lookup(place_ref[pl.ds(row, 1), :], low, high, row, total)
        return total

    place = lax.fori_loop(0, 8, find, jnp.zeros_like(cells))
    pos_ref[...] = place.reshape(pos_ref.shape)

    for copy in halos:
        copy.wait()

    shape = (4, 32, LANES)
    row_id = iota(shape, 1)
    lane_id = iota(shape, 2)
    inside = [
        (jnp.where(at > 0, 1.0, 0.0), jnp.where(at < count - 1, 1.0, 0.0))
        for at, count in ((gz, DEPTH), (gx, 4), (gy, 4))
    ]
    for field, ref in enumerate(fields):
        center = ref[...]
        layers = slice(field * 4, field * 4 + 4)
        z_low = (z_recv[0, field] * inside[0][0])[None]
        z_high = (z_recv[1, field] * inside[0][1])[None]
        x_low = (x_recv[0, layers, :] * inside[1][0])[:, None, :]
        x_high = (x_recv[1, layers, :] * inside[1][1])[:, None, :]
        y_edges = []
        for side in range(2):
            edge = y_recv[side, field : field + 1, :] * inside[2][side]
            y_edges.append(jnp.broadcast_to(edge, (LANES, LANES)).T.reshape(shape))
        lower = (
            jnp.concatenate([z_low, center[:3]], axis=0),
            jnp.where(row_id == 0, x_low, pltpu.roll(center, 1, 1)),
            jnp.where(lane_id == 0, y_edges[0], pltpu.roll(center, 1, 2)),
        )
        upper = (
            jnp.concatenate([center[1:], z_high], axis=0),
            jnp.where(row_id == 31, x_high, pltpu.roll(center, 31, 1)),
            jnp.where(lane_id == LANES - 1, y_edges[1], pltpu.roll(center, LANES - 1, 2)),
        )
        total = center
        for axis in range(3):
            courant = vel_ref[axis]
            total = total + diffusion * (lower[axis] + upper[axis] - 2.0 * center)
            total = total - jnp.maximum(courant, 0.0) * (center - lower[axis])
            total = total - jnp.minimum(courant, 0.0) * (upper[axis] - center)
        swept_ref[field] = total
        value_ref[field] = total.reshape(LANES, LANES)

    bf16 = jnp.bfloat16

    def small(values):
        return values.astype(jnp.float32).astype(bf16)

    fine_row = small(iota((2 * LANES, LANES), 0))
    row_half = small(iota((64, LANES), 0) >> 1)
    even = (iota((16, LANES), 0) & 1) == 0

    def gather_sums(step, total):
        rows = pl.ds(pl.multiple_of(step * 8, 8), 8)
        place = pos_ref[step // 4, pl.ds(pl.multiple_of(lax.rem(step, 4) * 8, 8), 8), :]
        coarse_place = (place >> 8).astype(jnp.float32)
        fine_place = (place & 255).astype(jnp.float32)
        first = value_ref[0, rows, :]
        second = value_ref[1, rows, :]
        left, right = [], []
        for row in range(8):
            one = slice(row, row + 1)
            value = jnp.where(even, first[one], second[one])
            coarse = value.astype(bf16)
            rest = (value - coarse.astype(jnp.float32)).astype(bf16)
            tall = jnp.broadcast_to(coarse_place[one], (16, LANES)).astype(bf16)
            hit = jnp.concatenate([tall] * 4, axis=0) == row_half
            zero = jnp.zeros((64, LANES), bf16)
            left.append(
                jnp.concatenate(
                    [
                        jnp.where(hit, jnp.concatenate([coarse] * 4, axis=0), zero),
                        jnp.where(hit, jnp.concatenate([rest] * 4, axis=0), zero),
                    ],
                    axis=0,
                )
            )
            tall = jnp.broadcast_to(fine_place[one], (16, LANES)).astype(bf16)
            hit = jnp.concatenate([tall] * 16, axis=0) == fine_row
            ones = jnp.ones((2 * LANES, LANES), bf16)
            right.append(jnp.where(hit, ones, jnp.zeros_like(ones)))
        return total + lax.dot_general(
            jnp.concatenate(left, axis=1),
            jnp.concatenate(right, axis=1),
            (((1,), (1,)), ((), ())),
            preferred_element_type=jnp.float32,
        )

    sums = lax.fori_loop(0, 16, gather_sums, jnp.zeros((LANES, 2 * LANES), jnp.float32))
    sums_ref[...] = (sums[:64] + sums[64:]).reshape(COLS, 4, 2 * LANES)

    send(1, col_ids, lambda number: sums_ref.at[col_peers[number]], a_recv.at[column])
    a_recv[column] = sums_ref[column]

    state_ref[SLOTS] = jnp.zeros((AGES, SIZES), jnp.float32)
    for slot in range(SLOTS + 1):
        ages_ref[slot : slot + 1, :] = jnp.sum(state_ref[slot], axis=0, keepdims=True)
    summed = ages_ref[...]
    owned = jnp.where(owner_dev == column * DEPTH + gz, 1.0, 0.0)
    held = jnp.sum(jnp.sum(owned, axis=0, keepdims=True), axis=1, keepdims=True)
    block = lax.rem(chip, 4)
    wide = (DEPTH, LANES)
    lane = iota(wide, 1)
    local = lane & 31
    slot_of_lane = jnp.where(core == 1, 31 - local, local)
    here = ((lane >> 5) == block) & (slot_of_lane == iota(wide, 0))
    here = here & (slot_of_lane.astype(jnp.float32) < held)
    masses = []
    for field in range(2):
        weighted = summed * weight_ref[field : field + 1, :]
        mass = jnp.sum(weighted, axis=1, keepdims=True) / (AGES * SIZES)
        masses.append(jnp.sum(jnp.where(here, mass, 0.0), axis=0, keepdims=True))
    packed = masses[0] + pltpu.roll(masses[1], 32, 1)
    bio_send[0] = packed
    bio_recv[gz] = packed
    send(0, deep_ids, lambda number: bio_send.at[0], bio_recv.at[gz])

    division = division_ref[...]
    turned_ref[0] = division
    for step in range(1, SUBSTEPS):
        turned_ref[step] = pltpu.roll(division, AGES - step, 0)
    turned_out = pltpu.make_async_copy(turned_ref, turned_hbm, local_sem.at[3])
    turned_out.start()

    arrived(1, a_recv, COLS - 1)
    send_flows(1)
    part = jnp.sum(a_recv[...], axis=0)
    split = []
    for field in range(2):
        split.append(
            jnp.concatenate(
                [
                    part[2 * (row // 2) + field : 2 * (row // 2) + field + 1][
                        :, (row % 2) * LANES : (row % 2 + 1) * LANES
                    ]
                    for row in range(4)
                ],
                axis=0,
            )
        )

    first_core = core == 0
    pair_send[0] = jnp.where(first_core, split[1], split[0])
    send(2, [sibling], lambda number: pair_send.at[0], pair_recv.at[0])
    arrived(2, pair_recv, 1)
    chip_sum = jnp.where(first_core, split[0], split[1]) + pair_recv[0]
    deep_send[0] = chip_sum
    send(3, same_core_ids, lambda number: deep_send.at[0], deep_recv.at[chip])
    deep_recv[chip] = chip_sum
    arrived(3, deep_recv, 15)
    added = jnp.sum(deep_recv[...], axis=0)
    pair_send[1] = added
    send(4, [sibling], lambda number: pair_send.at[1], pair_recv.at[1])
    arrived(4, pair_recv, 1)
    other = pair_recv[1]
    mean_sub = jnp.where(first_core, added, other) / CELLS
    mean_oxy = jnp.where(first_core, other, added) / CELLS
    rate = growth_max * mean_sub / (half_substrate + mean_sub) * mean_oxy / (half_oxygen + mean_oxy)

    own_row = jnp.zeros((1, LANES), jnp.float32)
    for row in range(4):
        own_row = own_row + jnp.where(gz // 8 == row, rate[row : row + 1, :], 0.0)
    rate_row[...] = own_row
    to_scalar = pltpu.make_async_copy(rate_row, rate_smem, local_sem.at[4])
    to_scalar.start()

    arrived(0, bio_recv, DEPTH - 1)
    rows = bio_recv[...].reshape(DEPTH, LANES)
    mine = (lane >> 5) == ((iota(wide, 0) >> 1) & 3)
    for field in range(2):
        turned = rows if field == 0 else pltpu.roll(rows, LANES - 32, 1)
        kept = jnp.where(mine, turned, 0.0)
        for row in range(4):
            mass = jnp.sum(kept[8 * row : 8 * row + 8, :], axis=0, keepdims=True)
            at = field * 4 + row
            d_send[0, at : at + 1, :] = uptake_gain * rate[row : row + 1, :] * mass
    d_send[0, 8:12, :] = rate
    d_send[0, 12:16, :] = jnp.zeros((4, LANES), jnp.float32)
    send(5, col_ids, lambda number: d_send.at[0], d_recv.at[column])
    d_recv[column] = d_send[0]
    send_flows(2)

    to_scalar.wait()

    def rate_of(slot):
        return rate_smem[0, block * 32 + jnp.where(core == 1, 31 - slot, slot)]

    grow_rounds(state_ref, rate_of, mother_ref, turned_ref, growth_ref, daughter_ref, 4)

    state_out = pltpu.make_async_copy(state_ref, state_hbm, local_sem.at[5])
    state_out.start()

    arrived(5, d_recv, COLS - 1)
    rates = jnp.zeros((COLS, LANES), jnp.float32)
    for row in range(4):
        rates = rates + jnp.where(gz // 8 == row, d_recv[:, 8 + row, :], 0.0)
    rates_ref[...] = rates

    tables = []
    for field in range(2):
        for half in range(2):
            tables.append(
                jnp.concatenate(
                    [
                        d_recv[:, field * 4 + 2 * half, :],
                        d_recv[:, field * 4 + 2 * half + 1, :],
                    ],
                    axis=1,
                )
            )
    whole = jnp.concatenate(tables, axis=0)
    coarse_table = whole.astype(bf16)
    rest_table = (whole - coarse_table.astype(jnp.float32)).astype(bf16)
    both = jnp.concatenate([coarse_table, rest_table], axis=0)
    table_row = iota((COLS, LANES), 0)

    def draw(step, carry):
        rows = pl.ds(pl.multiple_of(step * 8, 8), 8)
        place = pos_ref[step // 4, pl.ds(pl.multiple_of(lax.rem(step, 4) * 8, 8), 8), :]
        fine_place = (place & 255).astype(jnp.float32)
        right = []
        for row in range(8):
            tall = jnp.broadcast_to(fine_place[row : row + 1], (16, LANES)).astype(bf16)
            hit = jnp.concatenate([tall] * 16, axis=0) == fine_row
            ones = jnp.ones((2 * LANES, LANES), bf16)
            right.append(jnp.where(hit, ones, jnp.zeros_like(ones)))
        found = jnp.dot(
            both, jnp.concatenate(right, axis=1), preferred_element_type=jnp.float32
        )
        found = found[:64] + found[64:]
        first, second = [], []
        for row in range(8):
            lanes = slice(row * LANES, (row + 1) * LANES)
            high = place[row : row + 1] >> 8
            for field, out in enumerate((first, second)):
                kept = jnp.zeros((COLS, LANES), jnp.float32)
                for half in range(2):
                    at = (field * 2 + half) * COLS
                    hit = high == 2 * table_row + half
                    kept = kept + jnp.where(hit, found[at : at + COLS, lanes], 0.0)
                out.append(jnp.sum(kept, axis=0, keepdims=True))
        value_ref[0, rows, :] = jnp.concatenate(first, axis=0)
        value_ref[1, rows, :] = jnp.concatenate(second, axis=0)
        return carry

    lax.fori_loop(0, 16, draw, 0)
    for field, half in enumerate((half_substrate, half_oxygen)):
        swept = swept_ref[field]
        drawn = value_ref[field].reshape(shape)
        fields_ref[field] = swept - drawn * swept / (half + swept)

    turned_out.wait()
    state_out.wait()
    left_here(0, bio_recv, DEPTH - 1)
    left_here(1, a_recv, COLS - 1)
    left_here(2, pair_recv, 1)
    left_here(3, deep_recv, 15)
    left_here(4, pair_recv, 1)
    left_here(5, d_recv, COLS - 1)
    stay.wait()
    for copy in flows:
        copy.wait()


def sweep(sub, oxy, velocity, cell_map, owner, weight, growth, daughter, division, flow, pop):
    f32 = jnp.float32
    shape = jax.ShapeDtypeStruct
    return pl.pallas_call(
        sweep_kernel,
        out_shape=(
            shape((2,) + sub.shape, f32),
            shape((1, LANES), jnp.int32),
            shape((COLS, LANES), f32),
            shape((SUBSTEPS, AGES, SIZES), f32),
            shape((SLOTS + 1, AGES, SIZES), f32),
            shape((COLS, 2 * AGES, SIZES), f32),
        ),
        in_specs=[HBM_SPEC] * 11,
        out_specs=(VMEM_SPEC,) * 3 + (HBM_SPEC,) * 3,
        scratch_shapes=[
            pltpu.VMEM((2,) + sub.shape, f32),
            pltpu.VMEM(sub.shape, jnp.int32),
            pltpu.VMEM((SUBSTEPS, AGES, SIZES), f32),
            pltpu.VMEM((SLOTS + 1, AGES, SIZES), f32),
            pltpu.VMEM((COLS, 2 * AGES, SIZES), f32),
            pltpu.VMEM(flow.shape, jnp.int32),
            pltpu.VMEM((64, LANES), jnp.int32),
            pltpu.VMEM((64, LANES), jnp.int32),
            pltpu.VMEM((64, LANES), f32),
            pltpu.SMEM((1, LANES), jnp.int32),
            pltpu.VMEM(sub.shape, f32),
            pltpu.VMEM(sub.shape, f32),
            pltpu.VMEM(velocity.shape, f32),
            pltpu.VMEM(sub.shape, jnp.int32),
            pltpu.VMEM((64, LANES), jnp.int32),
            pltpu.VMEM(weight.shape, f32),
            pltpu.VMEM(growth.shape, growth.dtype),
            pltpu.VMEM(daughter.shape, daughter.dtype),
            pltpu.VMEM(division.shape, f32),
            pltpu.VMEM((2, 8, LANES), f32),
            pltpu.VMEM((2, 8, LANES), f32),
            pltpu.VMEM((2, 2, LANES), f32),
            pltpu.VMEM((2, 2, LANES), f32),
            pltpu.VMEM((2, 2, 32, LANES), f32),
            pltpu.VMEM((64, LANES), jnp.int32),
            pltpu.VMEM((SLOTS + 1, SIZES), f32),
            pltpu.VMEM((SLOTS + 1, SIZES), f32),
            pltpu.VMEM((2, LANES, LANES), f32),
            pltpu.VMEM((COLS, 4, 2 * LANES), f32),
            pltpu.VMEM((COLS, 4, 2 * LANES), f32),
            pltpu.VMEM((2, 4, LANES), f32),
            pltpu.VMEM((2, 4, LANES), f32),
            pltpu.VMEM((1, 4, LANES), f32),
            pltpu.VMEM((16, 4, LANES), f32),
            pltpu.VMEM((1, 1, LANES), f32),
            pltpu.VMEM((DEPTH, 1, LANES), f32),
            pltpu.VMEM((1, 16, LANES), f32),
            pltpu.VMEM((COLS, 16, LANES), f32),
            pltpu.VMEM((1, LANES), f32),
            pltpu.SMEM((1, LANES), f32),
            pltpu.SemaphoreType.DMA((16,)),
            pltpu.SemaphoreType.DMA((8,)),
            pltpu.SemaphoreType.DMA((8,)),
            pltpu.SemaphoreType.DMA((COLS - 1,)),
            pltpu.SemaphoreType.DMA((COLS - 1,)),
            pltpu.SemaphoreType.DMA((6,)),
            pltpu.SemaphoreType.DMA((6,)),
        ],
        compiler_params=pltpu.CompilerParams(
            collective_id=0, has_side_effects=True, vmem_limit_bytes=VMEM_BYTES
        ),
        cost_estimate=pl.CostEstimate(
            flops=3_200_000_000, bytes_accessed=8_000_000, transcendentals=0
        ),
    )(sub, oxy, velocity, cell_map, owner, weight, growth, daughter, division, flow, pop)


def finish_kernel(
    list_ref,
    rate_table,
    flow_rate_ref,
    fields_hbm,
    own_hbm,
    growth_hbm,
    daughter_hbm,
    turned_hbm,
    incoming_ref,
    sub_out_ref,
    oxy_out_ref,
    pop_out_ref,
    own_ref,
    growth_ref,
    daughter_ref,
    turned_ref,
    state,
    mother_ref,
    rate_list,
    scale_of,
    own_scale,
    target_of,
    load_sem,
    state_sem,
):
    depth = lax.axis_index("gz")
    core = depth & 1
    block = (depth >> 1) & 3
    pairs = (
        (own_hbm, own_ref),
        (growth_hbm, growth_ref),
        (daughter_hbm, daughter_ref),
        (turned_hbm, turned_ref),
        (fields_hbm.at[0], sub_out_ref),
        (fields_hbm.at[1], oxy_out_ref),
    )
    loads = [
        pltpu.make_async_copy(source, target, load_sem.at[number])
        for number, (source, target) in enumerate(pairs)
    ]
    for copy in loads:
        copy.start()

    def scan_arriving(item, count):
        col, rank = item >> 1, item & 1
        lowest, highest = list_ref[0, col + 32], list_ref[0, col + 48]
        key = jnp.where(rank == 0, lowest, highest)
        valid = jnp.where(rank == 0, highest >= 0, highest > lowest)

        @pl.when(valid)
        def _():
            slot = key >> 9
            lane = block * 32 + jnp.where(core == 1, 31 - slot, slot)
            rate_list[count] = rate_table[col, lane]
            scale_of[count] = flow_rate_ref[key & 15]
            target_of[count] = (key >> 4) & 31
            pltpu.make_async_copy(
                incoming_ref.at[col, pl.ds(pl.multiple_of(rank * AGES, AGES), AGES)],
                state.at[count],
                state_sem.at[0],
            ).start()

        return count + jnp.where(valid, 1, 0)

    total = lax.fori_loop(0, 2 * COLS, scan_arriving, jnp.int32(0))

    def scan_own(col, count):
        lowest, highest = list_ref[0, col], list_ref[0, col + 16]

        @pl.when(highest >= 0)
        def _():
            own_scale[lowest >> 4] = flow_rate_ref[lowest & 15]
            own_scale[highest >> 4] = flow_rate_ref[highest & 15]

        return count + jnp.where(highest >= 0, 1, 0) + jnp.where(highest > lowest, 1, 0)

    own = lax.fori_loop(0, COLS, scan_own, jnp.int32(0))
    for copy in loads:
        copy.wait()

    top = AGES - SUBSTEPS
    for slot in range(SLOTS):

        @pl.when(slot < own)
        def _():
            kept = own_ref[slot]
            kept = kept - own_scale[slot] * kept
            pop_out_ref[slot, :SUBSTEPS, :] = kept[top:]
            pop_out_ref[slot, SUBSTEPS:, :] = kept[:top]

        @pl.when(slot >= own)
        def _():
            pop_out_ref[slot] = jnp.zeros((AGES, SIZES), jnp.float32)

    def fetched(slot, carry):
        pltpu.make_async_copy(
            incoming_ref.at[0, pl.ds(0, AGES)], state.at[slot], state_sem.at[0]
        ).wait()
        return carry

    lax.fori_loop(0, total, fetched, 0)
    grow_rounds(
        state,
        lambda slot: rate_list[slot],
        mother_ref,
        turned_ref,
        growth_ref,
        daughter_ref,
        (total + GROUP - 1) // GROUP,
    )

    def arrive(item, carry):
        slot = target_of[item]
        inflow = scale_of[item] * state[item]
        pop_out_ref[slot, :SUBSTEPS, :] = pop_out_ref[slot, :SUBSTEPS, :] + inflow[top:]
        pop_out_ref[slot, SUBSTEPS:, :] = pop_out_ref[slot, SUBSTEPS:, :] + inflow[:top]
        return carry

    lax.fori_loop(0, total, arrive, 0)


def finish(lists, rates, flow_rates, fields, state, growth, daughter, turned, incoming):
    f32 = jnp.float32
    field = jax.ShapeDtypeStruct(fields.shape[1:], f32)
    return pl.pallas_call(
        finish_kernel,
        out_shape=(field, field, jax.ShapeDtypeStruct((SLOTS, AGES, SIZES), f32)),
        in_specs=[SMEM_SPEC] * 3 + [HBM_SPEC] * 6,
        out_specs=(VMEM_SPEC,) * 3,
        scratch_shapes=[
            pltpu.VMEM(state.shape, f32),
            pltpu.VMEM(growth.shape, growth.dtype),
            pltpu.VMEM(daughter.shape, daughter.dtype),
            pltpu.VMEM(turned.shape, f32),
            pltpu.VMEM((SLOTS + 1, AGES, SIZES), f32),
            pltpu.VMEM((SLOTS + 1, SIZES), f32),
            pltpu.SMEM((32,), f32),
            pltpu.SMEM((32,), f32),
            pltpu.SMEM((32,), f32),
            pltpu.SMEM((32,), jnp.int32),
            pltpu.SemaphoreType.DMA((6,)),
            pltpu.SemaphoreType.DMA((1,)),
        ],
        compiler_params=pltpu.CompilerParams(vmem_limit_bytes=VMEM_BYTES),
        cost_estimate=pl.CostEstimate(
            flops=2_000_000_000, bytes_accessed=8_000_000, transcendentals=0
        ),
    )(lists, rates, flow_rates, fields, state, growth, daughter, turned, incoming)


def per_device(
    substrate,
    oxygen,
    velocity,
    cell_map,
    owner_slot,
    flow_list,
    flow_rates,
    population,
    growth,
    daughter_kernel,
    division_rate,
    uptake_weight,
):
    fields, lists, rates, turned, state, incoming = sweep(
        substrate,
        oxygen,
        velocity,
        cell_map,
        owner_slot.reshape(64, LANES),
        uptake_weight,
        growth,
        daughter_kernel,
        division_rate,
        flow_list,
        population,
    )
    return finish(
        lists, rates, flow_rates, fields, state, growth, daughter_kernel, turned, incoming
    )


def solution(mesh):
    return jax.shard_map(
        per_device,
        mesh=mesh,
        in_specs=(
            P("gz", "gx", "gy"),
            P("gz", "gx", "gy"),
            P(None, "gz", "gx", "gy"),
            P("gz", "gx", "gy"),
            P(),
            P(),
            P(),
            P(("gx", "gy", "gz"), None, None),
            P(),
            P(),
            P(),
            P(),
        ),
        out_specs=(P("gz", "gx", "gy"), P("gz", "gx", "gy"), P(("gx", "gy", "gz"), None, None)),
        check_vma=False,
    )
```

```python
import functools

import jax
import jax.numpy as jnp
from jax import lax
from jax.experimental import pallas as pl
from jax.experimental.pallas import tpu as pltpu
from jax.sharding import PartitionSpec as P

SUBSTEPS = 8
CELLS = 1024
SLOTS = 31
AGES = 64
SIZES = 256
COLS = 16
DEPTH = 32
LANES = 128
GROUP = 8
NONE_KEY = 65536.0

diffusion = 0.05
growth_max = 0.8
half_substrate = 0.3
half_oxygen = 0.1
uptake_gain = 3.0

FLOW_PARTS = (
    ((1, 0), (3, 0), (0, 1), (0, 3), (2, 0), (0, 2)),
    ((1, 1), (3, 3), (1, 3), (3, 1), (1, 2), (2, 1)),
    ((2, 3), (3, 2), (2, 2)),
)

MESH = pl.DeviceIdType.MESH
VMEM_SPEC = pl.BlockSpec(memory_space=pltpu.VMEM)
SMEM_SPEC = pl.BlockSpec(memory_space=pltpu.SMEM)
HBM_SPEC = pl.BlockSpec(memory_space=pltpu.HBM)
VMEM_BYTES = 66_900_000


def iota(shape, dim):
    return lax.broadcasted_iota(jnp.int32, shape, dim)


def device_of(slot):
    return (slot * 33826) >> 20


def lookup(table_row, index, high, row_id, total):
    row = jnp.broadcast_to(table_row, index.shape)
    found = jnp.take_along_axis(row, index, axis=1, mode="promise_in_bounds")
    return jnp.where(high == row_id, found, total)


def grow_rounds(
    state, rate_of, mother_ref, turned_ref, growth_ref, daughter_ref, groups, size
):
    for step in range(SUBSTEPS):
        oldest = AGES - 1 - step

        def one_group(group, carry, oldest=oldest, step=step):
            base = group * size
            held = state[pl.ds(base, size)]
            moved = jnp.dot(
                held.reshape(size * AGES, SIZES).astype(jnp.bfloat16),
                growth_ref[...],
                preferred_element_type=jnp.float32,
            ).reshape(size, AGES, SIZES)
            for slot in range(size):
                rate = rate_of(base + slot)
                grown = held[slot] + rate * (moved[slot] - held[slot])
                divided = (turned_ref[step] * rate) * grown
                remain = grown - divided
                mother_ref[pl.ds(base + slot, 1), :] = jnp.sum(divided, axis=0, keepdims=True)
                state[base + slot] = remain
                state[base + slot, oldest - 1 : oldest, :] = (
                    remain[oldest - 1 : oldest, :] + remain[oldest : oldest + 1, :]
                )
            return carry

        lax.fori_loop(0, groups, one_group, 0)
        newborn = 2.0 * jnp.dot(
            mother_ref[...].astype(jnp.bfloat16),
            daughter_ref[...],
            preferred_element_type=jnp.float32,
        )
        state[:, oldest, :] = newborn


def list_flows(me, owner_ref, flow_ref, target_ref, index_ref, row_ref):
    for row in range(64):
        lanes = slice(row * LANES, (row + 1) * LANES)
        target_ref[row : row + 1, :] = flow_ref[0:1, lanes]
        index_ref[row : row + 1, :] = flow_ref[1:2, lanes]
    owner = owner_ref[...]
    targets = target_ref[...]
    low, high = targets & 127, targets >> 7
    target_slot = jnp.zeros_like(owner)
    for row in range(64):
        target_slot = lookup(owner_ref[row : row + 1, :], low, high, row, target_slot)
    rate_index = index_ref[...]
    source_dev = device_of(owner)
    source_local = owner - source_dev * SLOTS
    target_dev = device_of(target_slot)
    target_local = target_slot - target_dev * SLOTS
    send_key = (source_local * 16 + rate_index).astype(jnp.float32)
    recv_key = (source_local * 512 + target_local * 16 + rate_index).astype(jnp.float32)
    send_col = jnp.where(source_dev == me, target_dev >> 5, -1)
    recv_col = jnp.where(target_dev == me, source_dev >> 5, -1)
    for col in range(COLS):
        for kind, (key, cols) in enumerate(((send_key, send_col), (recv_key, recv_col))):
            hit = cols == col
            low_row = jnp.min(jnp.where(hit, key, NONE_KEY), axis=0, keepdims=True)
            high_row = jnp.max(jnp.where(hit, key, -1.0), axis=0, keepdims=True)
            at = kind * 32 + col
            row_ref[at : at + 1, :] = low_row
            row_ref[at + 16 : at + 17, :] = high_row
    square = (64, LANES)
    rows = row_ref[...]
    is_low = (iota((64, 1), 0) & 16) == 0
    reduced = jnp.where(
        is_low, jnp.min(rows, axis=1, keepdims=True), jnp.max(rows, axis=1, keepdims=True)
    )
    diagonal = jnp.where(iota(square, 0) == iota(square, 1), reduced, 0.0)
    return jnp.sum(diagonal, axis=0, keepdims=True).astype(jnp.int32)


def sweep_kernel(
    sub_hbm,
    oxy_hbm,
    vel_hbm,
    map_hbm,
    owner_hbm,
    weight_hbm,
    growth_hbm,
    daughter_hbm,
    division_hbm,
    flow_hbm,
    pop_ref,
    fields_ref,
    list_ref,
    rates_ref,
    turned_hbm,
    state_hbm,
    incoming_ref,
    swept_ref,
    pos_ref,
    turned_ref,
    state_ref,
    payload_ref,
    flow_ref,
    target_ref,
    index_ref,
    row_ref,
    list_smem,
    sub_ref,
    oxy_ref,
    vel_ref,
    map_ref,
    owner_ref,
    weight_ref,
    growth_ref,
    daughter_ref,
    division_ref,
    x_send,
    x_recv,
    y_send,
    y_recv,
    z_recv,
    place_ref,
    ages_ref,
    mother_ref,
    value_ref,
    sums_ref,
    a_recv,
    pair_send,
    pair_recv,
    deep_send,
    deep_recv,
    bio_send,
    bio_recv,
    d_send,
    d_recv,
    rate_row,
    rate_smem,
    local_sem,
    halo_send_sem,
    halo_recv_sem,
    flow_send_sem,
    flow_recv_sem,
    send_sem,
    recv_sem,
):
    gx, gy, gz = lax.axis_index("gx"), lax.axis_index("gy"), lax.axis_index("gz")
    column = gx * 4 + gy
    chip, core = gz // 2, lax.rem(gz, 2)
    col_peers = [lax.rem(column + step, COLS) for step in range(1, COLS)]
    col_ids = [(peer // 4, lax.rem(peer, 4), gz) for peer in col_peers]
    deep_ids = [(gx, gy, lax.rem(gz + step, DEPTH)) for step in range(1, DEPTH)]
    same_core_ids = [(gx, gy, lax.rem(gz + step, DEPTH)) for step in range(2, DEPTH, 2)]
    sibling = (gx, gy, gz + 1 - 2 * core)

    pairs = (
        (sub_hbm, sub_ref),
        (oxy_hbm, oxy_ref),
        (map_hbm, map_ref),
        (owner_hbm, owner_ref),
        (weight_hbm, weight_ref),
        (division_hbm, division_ref),
        (vel_hbm, vel_ref),
        (growth_hbm, growth_ref),
        (daughter_hbm, daughter_ref),
        (flow_hbm, flow_ref),
    )
    loads = [
        pltpu.make_async_copy(source, target, local_sem.at[6 + number])
        for number, (source, target) in enumerate(pairs)
    ]
    for copy in loads:
        copy.start()
    barrier = pltpu.get_barrier_semaphore()
    for peer in col_ids + deep_ids:
        pl.semaphore_signal(barrier, inc=1, device_id=peer, device_id_type=MESH)
    load = pltpu.make_async_copy(pop_ref, state_ref.at[pl.ds(0, SLOTS)], local_sem.at[0])
    load.start()

    def send(stage, ids, source_of, target):
        for number, device in enumerate(ids):
            pltpu.make_async_remote_copy(
                src_ref=source_of(number),
                dst_ref=target,
                send_sem=send_sem.at[stage],
                recv_sem=recv_sem.at[stage],
                device_id=device,
                device_id_type=MESH,
            ).start()

    def arrived(stage, buffer, count):
        part = buffer.at[pl.ds(0, count)]
        pltpu.make_async_copy(part, part, recv_sem.at[stage]).wait()

    def left_here(stage, buffer, count):
        part = buffer.at[pl.ds(0, count)]
        pltpu.make_async_copy(part, part, send_sem.at[stage]).wait()

    flows = []

    def send_flows(part):
        for step_x, step_y in FLOW_PARTS[part]:
            near_x, near_y = lax.rem(gx + step_x, 4), lax.rem(gy + step_y, 4)
            number = len(flows)
            copy = pltpu.make_async_remote_copy(
                src_ref=payload_ref.at[near_x * 4 + near_y],
                dst_ref=incoming_ref.at[column],
                send_sem=flow_send_sem.at[number],
                recv_sem=flow_recv_sem.at[number],
                device_id=(near_x, near_y, gz),
                device_id_type=MESH,
            )
            copy.start()
            flows.append(copy)

    for copy in loads[:2]:
        copy.wait()
    fields = (sub_ref, oxy_ref)
    for field, ref in enumerate(fields):
        layers = slice(field * 4, field * 4 + 4)
        x_send[0, layers, :] = ref[:, 0, :]
        x_send[1, layers, :] = ref[:, 31, :]
        turned = ref[...].reshape(LANES, LANES).T
        y_send[0, field : field + 1, :] = turned[0:1, :]
        y_send[1, field : field + 1, :] = turned[LANES - 1 : LANES, :]

    for copy in loads[2:]:
        copy.wait()
    list_ref[...] = list_flows(
        column * DEPTH + gz, owner_ref, flow_ref, target_ref, index_ref, row_ref
    )
    list_copy = pltpu.make_async_copy(list_ref, list_smem, local_sem.at[1])
    list_copy.start()
    owner = owner_ref[...]
    owner_dev = device_of(owner)
    owner_local = owner - owner_dev * SLOTS
    place_ref[...] = (owner_dev >> 1) * 32 + jnp.where(
        (owner_dev & 1) == 1, 31 - owner_local, owner_local
    )
    pl.semaphore_wait(barrier, len(col_ids) + len(deep_ids))

    halos = []
    for side in range(2):
        step = 3 if side == 0 else 1
        near_x = (lax.rem(gx + step, 4), gy, gz)
        near_y = (gx, lax.rem(gy + step, 4), gz)
        near_z = (gx, gy, lax.rem(gz + (DEPTH - 1 if side == 0 else 1), DEPTH))
        layer = 0 if side == 0 else 3
        pairs = [
            (x_send.at[side], x_recv.at[1 - side], near_x),
            (y_send.at[side], y_recv.at[1 - side], near_y),
            (sub_ref.at[layer], z_recv.at[1 - side, 0], near_z),
            (oxy_ref.at[layer], z_recv.at[1 - side, 1], near_z),
        ]
        for number, (source, target, device) in enumerate(pairs):
            sem = side * 4 + number
            halos.append(
                pltpu.make_async_remote_copy(
                    src_ref=source,
                    dst_ref=target,
                    send_sem=halo_send_sem.at[sem],
                    recv_sem=halo_recv_sem.at[sem],
                    device_id=device,
                    device_id_type=MESH,
                )
            )
    for copy in halos:
        copy.start()

    load.wait()
    list_copy.wait()

    def pack(col, carry):
        lowest, highest = list_smem[0, col], list_smem[0, col + 16]
        first = jnp.where(highest >= 0, (lowest >> 4) & 31, 0)
        second = jnp.where(highest >= 0, (highest >> 4) & 31, 0)
        payload_ref[col, :AGES, :] = state_ref[first]
        payload_ref[col, AGES:, :] = state_ref[second]
        return carry

    lax.fori_loop(0, COLS, pack, 0)
    stay = pltpu.make_async_copy(
        payload_ref.at[column], incoming_ref.at[column], local_sem.at[2]
    )
    stay.start()
    send_flows(0)

    bf16 = jnp.bfloat16

    def small(values):
        return values.astype(jnp.float32).astype(bf16)

    fine_row = small(iota((2 * LANES, LANES), 0))
    places = jnp.concatenate(
        [place_ref[pl.ds(0, 32, stride=2), :], place_ref[pl.ds(1, 32, stride=2), :]], axis=1
    )
    pieces = jnp.concatenate([small(places & ~127), small(places & 127)], axis=0)
    piece_row = iota((32, LANES), 0)

    def find(step, carry):
        rows = pl.ds(pl.multiple_of(lax.rem(step, 4) * 8, 8), 8)
        cells = map_ref[step // 4, rows, :]
        fine_cell = (cells & 255).astype(jnp.float32)
        right = []
        for row in range(8):
            tall = jnp.broadcast_to(fine_cell[row : row + 1], (16, LANES)).astype(bf16)
            hit = jnp.concatenate([tall] * 16, axis=0) == fine_row
            ones = jnp.ones((2 * LANES, LANES), bf16)
            right.append(jnp.where(hit, ones, jnp.zeros_like(ones)))
        found = jnp.dot(
            pieces, jnp.concatenate(right, axis=1), preferred_element_type=jnp.float32
        )
        found = found[:32] + found[32:]
        lines = []
        for row in range(8):
            hit = (cells[row : row + 1] >> 8) == piece_row
            kept = jnp.where(hit, found[:, row * LANES : (row + 1) * LANES], 0.0)
            lines.append(jnp.sum(kept, axis=0, keepdims=True))
        pos_ref[step // 4, rows, :] = jnp.concatenate(lines, axis=0).astype(jnp.int32)
        return carry

    lax.fori_loop(0, 16, find, 0)

    for copy in halos:
        copy.wait()

    shape = (4, 32, LANES)
    row_id = iota(shape, 1)
    lane_id = iota(shape, 2)
    inside = [
        (jnp.where(at > 0, 1.0, 0.0), jnp.where(at < count - 1, 1.0, 0.0))
        for at, count in ((gz, DEPTH), (gx, 4), (gy, 4))
    ]
    for field, ref in enumerate(fields):
        center = ref[...]
        layers = slice(field * 4, field * 4 + 4)
        z_low = (z_recv[0, field] * inside[0][0])[None]
        z_high = (z_recv[1, field] * inside[0][1])[None]
        x_low = (x_recv[0, layers, :] * inside[1][0])[:, None, :]
        x_high = (x_recv[1, layers, :] * inside[1][1])[:, None, :]
        y_edges = []
        for side in range(2):
            edge = y_recv[side, field : field + 1, :] * inside[2][side]
            y_edges.append(jnp.broadcast_to(edge, (LANES, LANES)).T.reshape(shape))
        lower = (
            jnp.concatenate([z_low, center[:3]], axis=0),
            jnp.where(row_id == 0, x_low, pltpu.roll(center, 1, 1)),
            jnp.where(lane_id == 0, y_edges[0], pltpu.roll(center, 1, 2)),
        )
        upper = (
            jnp.concatenate([center[1:], z_high], axis=0),
            jnp.where(row_id == 31, x_high, pltpu.roll(center, 31, 1)),
            jnp.where(lane_id == LANES - 1, y_edges[1], pltpu.roll(center, LANES - 1, 2)),
        )
        total = center
        for axis in range(3):
            courant = vel_ref[axis]
            total = total + diffusion * (lower[axis] + upper[axis] - 2.0 * center)
            total = total - jnp.maximum(courant, 0.0) * (center - lower[axis])
            total = total - jnp.minimum(courant, 0.0) * (upper[axis] - center)
        swept_ref[field] = total
        value_ref[field] = total.reshape(LANES, LANES)

    row_half = small(iota((64, LANES), 0) >> 1)
    even = (iota((16, LANES), 0) & 1) == 0

    def gather_sums(step, total):
        rows = pl.ds(pl.multiple_of(step * 8, 8), 8)
        place = pos_ref[step // 4, pl.ds(pl.multiple_of(lax.rem(step, 4) * 8, 8), 8), :]
        coarse_place = (place >> 8).astype(jnp.float32)
        fine_place = (place & 255).astype(jnp.float32)
        first = value_ref[0, rows, :]
        second = value_ref[1, rows, :]
        left, right = [], []
        for row in range(8):
            one = slice(row, row + 1)
            value = jnp.where(even, first[one], second[one])
            coarse = value.astype(bf16)
            rest = (value - coarse.astype(jnp.float32)).astype(bf16)
            tall = jnp.broadcast_to(coarse_place[one], (16, LANES)).astype(bf16)
            hit = jnp.concatenate([tall] * 4, axis=0) == row_half
            zero = jnp.zeros((64, LANES), bf16)
            left.append(
                jnp.concatenate(
                    [
                        jnp.where(hit, jnp.concatenate([coarse] * 4, axis=0), zero),
                        jnp.where(hit, jnp.concatenate([rest] * 4, axis=0), zero),
                    ],
                    axis=0,
                )
            )
            tall = jnp.broadcast_to(fine_place[one], (16, LANES)).astype(bf16)
            hit = jnp.concatenate([tall] * 16, axis=0) == fine_row
            ones = jnp.ones((2 * LANES, LANES), bf16)
            right.append(jnp.where(hit, ones, jnp.zeros_like(ones)))
        return total + lax.dot_general(
            jnp.concatenate(left, axis=1),
            jnp.concatenate(right, axis=1),
            (((1,), (1,)), ((), ())),
            preferred_element_type=jnp.float32,
        )

    sums = lax.fori_loop(0, 16, gather_sums, jnp.zeros((LANES, 2 * LANES), jnp.float32))
    sums_ref[...] = (sums[:64] + sums[64:]).reshape(COLS, 4, 2 * LANES)

    send(1, col_ids, lambda number: sums_ref.at[col_peers[number]], a_recv.at[column])
    a_recv[column] = sums_ref[column]

    state_ref[SLOTS] = jnp.zeros((AGES, SIZES), jnp.float32)
    for slot in range(SLOTS + 1):
        ages_ref[slot : slot + 1, :] = jnp.sum(state_ref[slot], axis=0, keepdims=True)
    summed = ages_ref[...]
    owned = jnp.where(owner_dev == column * DEPTH + gz, 1.0, 0.0)
    held = jnp.sum(jnp.sum(owned, axis=0, keepdims=True), axis=1, keepdims=True)
    block = lax.rem(chip, 4)
    wide = (DEPTH, LANES)
    lane = iota(wide, 1)
    local = lane & 31
    slot_of_lane = jnp.where(core == 1, 31 - local, local)
    here = ((lane >> 5) == block) & (slot_of_lane == iota(wide, 0))
    here = here & (slot_of_lane.astype(jnp.float32) < held)
    masses = []
    for field in range(2):
        weighted = summed * weight_ref[field : field + 1, :]
        mass = jnp.sum(weighted, axis=1, keepdims=True) / (AGES * SIZES)
        masses.append(jnp.sum(jnp.where(here, mass, 0.0), axis=0, keepdims=True))
    packed = masses[0] + pltpu.roll(masses[1], 32, 1)
    bio_send[0] = packed
    bio_recv[gz] = packed
    send(0, deep_ids, lambda number: bio_send.at[0], bio_recv.at[gz])

    division = division_ref[...]
    turned_ref[0] = division
    for step in range(1, SUBSTEPS):
        turned_ref[step] = pltpu.roll(division, AGES - step, 0)
    turned_out = pltpu.make_async_copy(turned_ref, turned_hbm, local_sem.at[3])
    turned_out.start()

    arrived(1, a_recv, COLS - 1)
    send_flows(1)
    part = jnp.sum(a_recv[...], axis=0)
    split = []
    for field in range(2):
        split.append(
            jnp.concatenate(
                [
                    part[2 * (row // 2) + field : 2 * (row // 2) + field + 1][
                        :, (row % 2) * LANES : (row % 2 + 1) * LANES
                    ]
                    for row in range(4)
                ],
                axis=0,
            )
        )

    first_core = core == 0
    pair_send[0] = jnp.where(first_core, split[1], split[0])
    send(2, [sibling], lambda number: pair_send.at[0], pair_recv.at[0])
    arrived(2, pair_recv, 1)
    chip_sum = jnp.where(first_core, split[0], split[1]) + pair_recv[0]
    deep_send[0] = chip_sum
    send(3, same_core_ids, lambda number: deep_send.at[0], deep_recv.at[chip])
    deep_recv[chip] = chip_sum
    arrived(3, deep_recv, 15)
    added = jnp.sum(deep_recv[...], axis=0)
    pair_send[1] = added
    send(4, [sibling], lambda number: pair_send.at[1], pair_recv.at[1])
    arrived(4, pair_recv, 1)
    other = pair_recv[1]
    mean_sub = jnp.where(first_core, added, other) / CELLS
    mean_oxy = jnp.where(first_core, other, added) / CELLS
    rate = growth_max * mean_sub / (half_substrate + mean_sub) * mean_oxy / (half_oxygen + mean_oxy)

    own_row = jnp.zeros((1, LANES), jnp.float32)
    for row in range(4):
        own_row = own_row + jnp.where(gz // 8 == row, rate[row : row + 1, :], 0.0)
    rate_row[...] = own_row
    to_scalar = pltpu.make_async_copy(rate_row, rate_smem, local_sem.at[4])
    to_scalar.start()

    arrived(0, bio_recv, DEPTH - 1)
    rows = bio_recv[...].reshape(DEPTH, LANES)
    mine = (lane >> 5) == ((iota(wide, 0) >> 1) & 3)
    for field in range(2):
        turned = rows if field == 0 else pltpu.roll(rows, LANES - 32, 1)
        kept = jnp.where(mine, turned, 0.0)
        for row in range(4):
            mass = jnp.sum(kept[8 * row : 8 * row + 8, :], axis=0, keepdims=True)
            at = field * 4 + row
            d_send[0, at : at + 1, :] = uptake_gain * rate[row : row + 1, :] * mass
    d_send[0, 8:12, :] = rate
    d_send[0, 12:16, :] = jnp.zeros((4, LANES), jnp.float32)
    send(5, col_ids, lambda number: d_send.at[0], d_recv.at[column])
    d_recv[column] = d_send[0]
    send_flows(2)

    to_scalar.wait()

    def rate_of(slot):
        return rate_smem[0, block * 32 + jnp.where(core == 1, 31 - slot, slot)]

    grow_rounds(state_ref, rate_of, mother_ref, turned_ref, growth_ref, daughter_ref, 2, 16)

    state_out = pltpu.make_async_copy(state_ref, state_hbm, local_sem.at[5])
    state_out.start()

    arrived(5, d_recv, COLS - 1)
    rates = jnp.zeros((COLS, LANES), jnp.float32)
    for row in range(4):
        rates = rates + jnp.where(gz // 8 == row, d_recv[:, 8 + row, :], 0.0)
    rates_ref[...] = rates

    tables = []
    for field in range(2):
        for half in range(2):
            tables.append(
                jnp.concatenate(
                    [
                        d_recv[:, field * 4 + 2 * half, :],
                        d_recv[:, field * 4 + 2 * half + 1, :],
                    ],
                    axis=1,
                )
            )
    whole = jnp.concatenate(tables, axis=0)
    coarse_table = whole.astype(bf16)
    rest_table = (whole - coarse_table.astype(jnp.float32)).astype(bf16)
    both = jnp.concatenate([coarse_table, rest_table], axis=0)
    table_row = iota((COLS, LANES), 0)

    def draw(step, carry):
        rows = pl.ds(pl.multiple_of(step * 8, 8), 8)
        place = pos_ref[step // 4, pl.ds(pl.multiple_of(lax.rem(step, 4) * 8, 8), 8), :]
        fine_place = (place & 255).astype(jnp.float32)
        right = []
        for row in range(8):
            tall = jnp.broadcast_to(fine_place[row : row + 1], (16, LANES)).astype(bf16)
            hit = jnp.concatenate([tall] * 16, axis=0) == fine_row
            ones = jnp.ones((2 * LANES, LANES), bf16)
            right.append(jnp.where(hit, ones, jnp.zeros_like(ones)))
        found = jnp.dot(
            both, jnp.concatenate(right, axis=1), preferred_element_type=jnp.float32
        )
        found = found[:64] + found[64:]
        first, second = [], []
        for row in range(8):
            lanes = slice(row * LANES, (row + 1) * LANES)
            high = place[row : row + 1] >> 8
            for field, out in enumerate((first, second)):
                kept = jnp.zeros((COLS, LANES), jnp.float32)
                for half in range(2):
                    at = (field * 2 + half) * COLS
                    hit = high == 2 * table_row + half
                    kept = kept + jnp.where(hit, found[at : at + COLS, lanes], 0.0)
                out.append(jnp.sum(kept, axis=0, keepdims=True))
        value_ref[0, rows, :] = jnp.concatenate(first, axis=0)
        value_ref[1, rows, :] = jnp.concatenate(second, axis=0)
        return carry

    lax.fori_loop(0, 16, draw, 0)
    for field, half in enumerate((half_substrate, half_oxygen)):
        swept = swept_ref[field]
        drawn = value_ref[field].reshape(shape)
        fields_ref[field] = swept - drawn * swept / (half + swept)

    turned_out.wait()
    state_out.wait()
    left_here(0, bio_recv, DEPTH - 1)
    left_here(1, a_recv, COLS - 1)
    left_here(2, pair_recv, 1)
    left_here(3, deep_recv, 15)
    left_here(4, pair_recv, 1)
    left_here(5, d_recv, COLS - 1)
    stay.wait()
    for copy in flows:
        copy.wait()


def sweep(sub, oxy, velocity, cell_map, owner, weight, growth, daughter, division, flow, pop):
    f32 = jnp.float32
    shape = jax.ShapeDtypeStruct
    return pl.pallas_call(
        sweep_kernel,
        out_shape=(
            shape((2,) + sub.shape, f32),
            shape((1, LANES), jnp.int32),
            shape((COLS, LANES), f32),
            shape((SUBSTEPS, AGES, SIZES), f32),
            shape((SLOTS + 1, AGES, SIZES), f32),
            shape((COLS, 2 * AGES, SIZES), f32),
        ),
        in_specs=[HBM_SPEC] * 11,
        out_specs=(VMEM_SPEC,) * 3 + (HBM_SPEC,) * 3,
        scratch_shapes=[
            pltpu.VMEM((2,) + sub.shape, f32),
            pltpu.VMEM(sub.shape, jnp.int32),
            pltpu.VMEM((SUBSTEPS, AGES, SIZES), f32),
            pltpu.VMEM((SLOTS + 1, AGES, SIZES), f32),
            pltpu.VMEM((COLS, 2 * AGES, SIZES), f32),
            pltpu.VMEM(flow.shape, jnp.int32),
            pltpu.VMEM((64, LANES), jnp.int32),
            pltpu.VMEM((64, LANES), jnp.int32),
            pltpu.VMEM((64, LANES), f32),
            pltpu.SMEM((1, LANES), jnp.int32),
            pltpu.VMEM(sub.shape, f32),
            pltpu.VMEM(sub.shape, f32),
            pltpu.VMEM(velocity.shape, f32),
            pltpu.VMEM(sub.shape, jnp.int32),
            pltpu.VMEM((64, LANES), jnp.int32),
            pltpu.VMEM(weight.shape, f32),
            pltpu.VMEM(growth.shape, growth.dtype),
            pltpu.VMEM(daughter.shape, daughter.dtype),
            pltpu.VMEM(division.shape, f32),
            pltpu.VMEM((2, 8, LANES), f32),
            pltpu.VMEM((2, 8, LANES), f32),
            pltpu.VMEM((2, 2, LANES), f32),
            pltpu.VMEM((2, 2, LANES), f32),
            pltpu.VMEM((2, 2, 32, LANES), f32),
            pltpu.VMEM((64, LANES), jnp.int32),
            pltpu.VMEM((SLOTS + 1, SIZES), f32),
            pltpu.VMEM((SLOTS + 1, SIZES), f32),
            pltpu.VMEM((2, LANES, LANES), f32),
            pltpu.VMEM((COLS, 4, 2 * LANES), f32),
            pltpu.VMEM((COLS, 4, 2 * LANES), f32),
            pltpu.VMEM((2, 4, LANES), f32),
            pltpu.VMEM((2, 4, LANES), f32),
            pltpu.VMEM((1, 4, LANES), f32),
            pltpu.VMEM((16, 4, LANES), f32),
            pltpu.VMEM((1, 1, LANES), f32),
            pltpu.VMEM((DEPTH, 1, LANES), f32),
            pltpu.VMEM((1, 16, LANES), f32),
            pltpu.VMEM((COLS, 16, LANES), f32),
            pltpu.VMEM((1, LANES), f32),
            pltpu.SMEM((1, LANES), f32),
            pltpu.SemaphoreType.DMA((16,)),
            pltpu.SemaphoreType.DMA((8,)),
            pltpu.SemaphoreType.DMA((8,)),
            pltpu.SemaphoreType.DMA((COLS - 1,)),
            pltpu.SemaphoreType.DMA((COLS - 1,)),
            pltpu.SemaphoreType.DMA((6,)),
            pltpu.SemaphoreType.DMA((6,)),
        ],
        compiler_params=pltpu.CompilerParams(
            collective_id=0, has_side_effects=True, vmem_limit_bytes=VMEM_BYTES
        ),
        cost_estimate=pl.CostEstimate(
            flops=3_200_000_000, bytes_accessed=8_000_000, transcendentals=0
        ),
    )(sub, oxy, velocity, cell_map, owner, weight, growth, daughter, division, flow, pop)


def finish_kernel(
    list_ref,
    rate_table,
    flow_rate_ref,
    fields_hbm,
    own_hbm,
    growth_hbm,
    daughter_hbm,
    turned_hbm,
    incoming_ref,
    sub_out_ref,
    oxy_out_ref,
    pop_out_ref,
    own_ref,
    growth_ref,
    daughter_ref,
    turned_ref,
    state,
    mother_ref,
    rate_list,
    scale_of,
    own_scale,
    target_of,
    load_sem,
    state_sem,
):
    depth = lax.axis_index("gz")
    core = depth & 1
    block = (depth >> 1) & 3
    pairs = (
        (own_hbm, own_ref),
        (growth_hbm, growth_ref),
        (daughter_hbm, daughter_ref),
        (turned_hbm, turned_ref),
        (fields_hbm.at[0], sub_out_ref),
        (fields_hbm.at[1], oxy_out_ref),
    )
    loads = [
        pltpu.make_async_copy(source, target, load_sem.at[number])
        for number, (source, target) in enumerate(pairs)
    ]
    for copy in loads:
        copy.start()

    def scan_arriving(item, count):
        col, rank = item >> 1, item & 1
        lowest, highest = list_ref[0, col + 32], list_ref[0, col + 48]
        key = jnp.where(rank == 0, lowest, highest)
        valid = jnp.where(rank == 0, highest >= 0, highest > lowest)

        @pl.when(valid)
        def _():
            slot = key >> 9
            lane = block * 32 + jnp.where(core == 1, 31 - slot, slot)
            rate_list[count] = rate_table[col, lane]
            scale_of[count] = flow_rate_ref[key & 15]
            target_of[count] = (key >> 4) & 31
            pltpu.make_async_copy(
                incoming_ref.at[col, pl.ds(pl.multiple_of(rank * AGES, AGES), AGES)],
                state.at[count],
                state_sem.at[0],
            ).start()

        return count + jnp.where(valid, 1, 0)

    total = lax.fori_loop(0, 2 * COLS, scan_arriving, jnp.int32(0))

    def scan_own(col, count):
        lowest, highest = list_ref[0, col], list_ref[0, col + 16]

        @pl.when(highest >= 0)
        def _():
            own_scale[lowest >> 4] = flow_rate_ref[lowest & 15]
            own_scale[highest >> 4] = flow_rate_ref[highest & 15]

        return count + jnp.where(highest >= 0, 1, 0) + jnp.where(highest > lowest, 1, 0)

    own = lax.fori_loop(0, COLS, scan_own, jnp.int32(0))
    for copy in loads:
        copy.wait()

    top = AGES - SUBSTEPS
    for slot in range(SLOTS):

        @pl.when(slot < own)
        def _():
            kept = own_ref[slot]
            kept = kept - own_scale[slot] * kept
            pop_out_ref[slot, :SUBSTEPS, :] = kept[top:]
            pop_out_ref[slot, SUBSTEPS:, :] = kept[:top]

        @pl.when(slot >= own)
        def _():
            pop_out_ref[slot] = jnp.zeros((AGES, SIZES), jnp.float32)

    def fetched(slot, carry):
        pltpu.make_async_copy(
            incoming_ref.at[0, pl.ds(0, AGES)], state.at[slot], state_sem.at[0]
        ).wait()
        return carry

    lax.fori_loop(0, total, fetched, 0)
    grow_rounds(
        state,
        lambda slot: rate_list[slot],
        mother_ref,
        turned_ref,
        growth_ref,
        daughter_ref,
        (total + GROUP - 1) // GROUP,
        GROUP,
    )

    def arrive(item, carry):
        slot = target_of[item]
        inflow = scale_of[item] * state[item]
        pop_out_ref[slot, :SUBSTEPS, :] = pop_out_ref[slot, :SUBSTEPS, :] + inflow[top:]
        pop_out_ref[slot, SUBSTEPS:, :] = pop_out_ref[slot, SUBSTEPS:, :] + inflow[:top]
        return carry

    lax.fori_loop(0, total, arrive, 0)


def finish(lists, rates, flow_rates, fields, state, growth, daughter, turned, incoming):
    f32 = jnp.float32
    field = jax.ShapeDtypeStruct(fields.shape[1:], f32)
    return pl.pallas_call(
        finish_kernel,
        out_shape=(field, field, jax.ShapeDtypeStruct((SLOTS, AGES, SIZES), f32)),
        in_specs=[SMEM_SPEC] * 3 + [HBM_SPEC] * 6,
        out_specs=(VMEM_SPEC,) * 3,
        scratch_shapes=[
            pltpu.VMEM(state.shape, f32),
            pltpu.VMEM(growth.shape, growth.dtype),
            pltpu.VMEM(daughter.shape, daughter.dtype),
            pltpu.VMEM(turned.shape, f32),
            pltpu.VMEM((SLOTS + 1, AGES, SIZES), f32),
            pltpu.VMEM((SLOTS + 1, SIZES), f32),
            pltpu.SMEM((32,), f32),
            pltpu.SMEM((32,), f32),
            pltpu.SMEM((32,), f32),
            pltpu.SMEM((32,), jnp.int32),
            pltpu.SemaphoreType.DMA((6,)),
            pltpu.SemaphoreType.DMA((1,)),
        ],
        compiler_params=pltpu.CompilerParams(vmem_limit_bytes=VMEM_BYTES),
        cost_estimate=pl.CostEstimate(
            flops=2_000_000_000, bytes_accessed=8_000_000, transcendentals=0
        ),
    )(lists, rates, flow_rates, fields, state, growth, daughter, turned, incoming)


def per_device(
    substrate,
    oxygen,
    velocity,
    cell_map,
    owner_slot,
    flow_list,
    flow_rates,
    population,
    growth,
    daughter_kernel,
    division_rate,
    uptake_weight,
):
    fields, lists, rates, turned, state, incoming = sweep(
        substrate,
        oxygen,
        velocity,
        cell_map,
        owner_slot.reshape(64, LANES),
        uptake_weight,
        growth,
        daughter_kernel,
        division_rate,
        flow_list,
        population,
    )
    return finish(
        lists, rates, flow_rates, fields, state, growth, daughter_kernel, turned, incoming
    )


def solution(mesh):
    return jax.shard_map(
        per_device,
        mesh=mesh,
        in_specs=(
            P("gz", "gx", "gy"),
            P("gz", "gx", "gy"),
            P(None, "gz", "gx", "gy"),
            P("gz", "gx", "gy"),
            P(),
            P(),
            P(),
            P(("gx", "gy", "gz"), None, None),
            P(),
            P(),
            P(),
            P(),
        ),
        out_specs=(P("gz", "gx", "gy"), P("gz", "gx", "gy"), P(("gx", "gy", "gz"), None, None)),
        check_vma=False,
    )
```
